512 devices in a mesh: space: 64 (over z, y), rep: 8 (over x, core).
Axes of the slice: x: 4, y: 4, z: 16, core: 2. Of those that a mesh axis runs over, the one named last changes fastest.
Arguments:
- feats: bfloat16 [512, 96, 512], P(('space', 'rep')), may hold values from -6 to 6
- cotangent: bfloat16 [512, 96, 512], P(('space', 'rep')), may hold values from -6 to 6
- occupancy: int32 [512, 512], P(('space', 'rep')), may hold values 0 or 1
- counts: int32 [512, 1], P(('space', 'rep')), may hold values from 1 to 1, as said below
- adjacency: int32 [512, 27], P(('space', 'rep')), may hold values from -1 to 511, as said below
- w_first: bfloat16 [96, 2592], replicated, may hold values from -0.125 to 0.125
- w_second: bfloat16 [96, 2592], replicated, may hold values from -0.125 to 0.125
Outputs:
- out_feats: bfloat16 [512, 96, 512], P(('space', 'rep'))
- grad_feats: bfloat16 [512, 96, 512], P(('space', 'rep'))
- grad_first: float32 [96, 2592], replicated
- grad_second: float32 [96, 2592], replicated
The draws below stay inside these ranges and needn't reach their ends.
Inputs may be any that keep to these rules, and one draw needn't show every extreme that they name: `counts`: the live slots of a device are its slots 0 to count - 1; some device has 1 live slots. `adjacency`: each device owns a region of 2 x 2 x 2 block sites of a map two sites high; the owners' regions form a square grid in which space index s sits at column s % q and row s // q, q * q being the size of the space axis. Entry k of a live block's row is the live block at the site moved by (k // 9 - 1, k // 3 % 3 - 1, k % 3 - 1), or -1 where no live block is there; entry 13 is the block itself. Rows of dead slots are -1. A named block has the same rep index, and its owner is the device itself or one of the at most eight owners beside it in the grid.
All inputs are finite; a program needn't handle non-finite values. No bound on the sum of `occupancy` on one device may be relied on, other than what follows from the above.
Results may differ from the reference program's by a relative error of at most 0.0029.
Values may be sent and summed in bfloat16 or wider, within the bound.
No kernel may reach another device: no remote copies, remote signals or barrier semaphores. Data moves between devices by JAX's collectives and lax.ppermute only.
A program may use at most 64 MiB of HBM per device.

```python
import math
import jax
import jax.numpy as jnp
from jax import lax

C = 96
BE = 8
BV = 512
NB = 1
BLOCKS = 512
N_SPACE = 64
N_REP = 8


OFFSETS = [(ax_a, ax_b, ax_c) for ax_a in (-1, 0, 1) for ax_b in (-1, 0, 1) for ax_c in (-1, 0, 1)]


def block_layout(key):
    grid_side = math.isqrt(N_SPACE)
    devices = N_SPACE * N_REP
    key_count, key_site, key_force = jax.random.split(key, 3)
    counts = jax.random.randint(key_count, (devices,), 1, NB + 1)
    forced = jax.random.randint(key_force, (), 0, devices)
    counts = counts.at[forced].set(NB)
    scores = jax.random.randint(key_site, (devices, 8), 0, 2 ** 20) * 8 + jnp.arange(8)[None, :]
    chosen = jnp.argsort(scores, axis=1)[:, :NB]
    device_ids = jnp.arange(devices)
    space_ids = device_ids // N_REP
    rep_ids = device_ids % N_REP
    cell_x = 2 * (space_ids % grid_side)[:, None] + chosen // 4
    cell_y = 2 * (space_ids // grid_side)[:, None] + chosen // 2 % 2
    cell_z = chosen % 2
    live_slots = jnp.arange(NB)[None, :] < counts[:, None]
    block_ids = device_ids[:, None] * NB + jnp.arange(NB)[None, :]
    lattice = jnp.full((N_REP, 2 * grid_side + 2, 2 * grid_side + 2, 4), -1, jnp.int32)
    rep_grid = jnp.broadcast_to(rep_ids[:, None], cell_x.shape)
    lattice = lattice.at[rep_grid, cell_x + 1, cell_y + 1, cell_z + 1].set(jnp.where(live_slots, block_ids, -1).astype(jnp.int32))
    neighbours = []
    for shift_x, shift_y, shift_z in OFFSETS:
        neighbours.append(lattice[rep_grid, cell_x + 1 + shift_x, cell_y + 1 + shift_y, cell_z + 1 + shift_z])
    adjacency = jnp.where(live_slots[..., None], jnp.stack(neighbours, axis=-1), -1)
    return (counts.reshape(devices, 1).astype(jnp.int32), adjacency.reshape(BLOCKS, 27).astype(jnp.int32))


def draw_counts(key, part):
    shared = block_layout(key)
    key = jax.random.fold_in(key, 11)
    return shared[0]


def draw_adjacency(key, part):
    shared = block_layout(key)
    key = jax.random.fold_in(key, 12)
    return shared[1]


def place_ends(entries, rng, low, largest):
    spot = [jax.random.randint(jax.random.fold_in(rng, axis), (), 0, length) for axis, length in enumerate(entries.shape)]
    widest = entries.shape.index(max(entries.shape))
    neighbour = spot[:widest] + [(spot[widest] + 1) % entries.shape[widest]] + spot[widest + 1:]
    return entries.at[tuple(spot)].set(low).at[tuple(neighbour)].set(largest)


def block_levels(rng, dims, pieces, least, high):
    loudness = 1.0
    for axis_at, parts in pieces:
        draws = jax.random.uniform(jax.random.fold_in(jax.random.fold_in(rng, 6), axis_at), (parts,), jnp.float32, least / len(pieces), high / len(pieces))
        loudness = loudness * jnp.repeat(jnp.exp(draws), dims[axis_at] // parts).reshape((-1,) + (1,) * (len(dims) - 1 - axis_at))
    return loudness


def normal_values(stream_key, dims, spread, limit, shards=(), kind=jnp.bfloat16):
    level = block_levels(stream_key, dims, shards, -0.22, 0.18) if shards else 1.0
    result = jax.random.normal(stream_key, dims, jnp.float32) * spread * level
    return jnp.minimum(jnp.maximum(result, -limit), limit).astype(kind)


def setup_inputs(seed: int = 0) -> dict:
    seeds = jax.random.split(jax.random.key(seed), 8)
    return {
        "feats": normal_values(seeds[0], (BLOCKS, C, BV), 1.0, 6.0, ((0, 512),)),
        "cotangent": normal_values(seeds[1], (BLOCKS, C, BV), 1.0, 6.0, ((0, 512),)),
        "occupancy": place_ends((jax.random.randint(seeds[2], (BLOCKS, BV), 0, 2) < 1).astype(jnp.int32), jax.random.fold_in(seeds[2], 1), 0, 1),
        "counts": draw_counts(jax.random.fold_in(seeds[7], 71), 0),
        "adjacency": draw_adjacency(jax.random.fold_in(seeds[7], 71), 0),
        "w_first": normal_values(seeds[5], (C, 27 * C), (27 * C) ** -0.5, 0.125),
        "w_second": normal_values(seeds[6], (C, 27 * C), (27 * C) ** -0.5, 0.125),
    }


OFFSETS = [(ax_a, ax_b, ax_c) for ax_a in (-1, 0, 1) for ax_b in (-1, 0, 1) for ax_c in (-1, 0, 1)]

def side_piece(block, shift_x, shift_y, shift_z):
    if shift_x < 0:
        block = block[:, -1:]
    elif shift_x > 0:
        block = block[:, :1]
    if shift_y < 0:
        block = block[:, :, -1:]
    elif shift_y > 0:
        block = block[:, :, :1]
    if shift_z < 0:
        block = block[:, :, :, -1:]
    elif shift_z > 0:
        block = block[:, :, :, :1]
    return block

def padded_field(gathered):
    planes = []
    for shift_x in (-1, 0, 1):
        row_list = []
        for shift_y in (-1, 0, 1):
            cell_list = []
            for shift_z in (-1, 0, 1):
                offset_id = (shift_x + 1) * 9 + (shift_y + 1) * 3 + (shift_z + 1)
                cell_list.append(side_piece(gathered[offset_id], shift_x, shift_y, shift_z))
            row_list.append(jnp.concatenate(cell_list, axis=3))
        planes.append(jnp.concatenate(row_list, axis=2))
    return jnp.concatenate(planes, axis=1)

def columns(padded, cube_edge):
    channels = padded.shape[0]
    stacked = []
    for shift_x, shift_y, shift_z in OFFSETS:
        window = padded[:, 1 + shift_x:1 + shift_x + cube_edge, 1 + shift_y:1 + shift_y + cube_edge, 1 + shift_z:1 + shift_z + cube_edge]
        stacked.append(window.reshape(channels, cube_edge ** 3))
    return jnp.concatenate(stacked, axis=0)

def block_columns(whole_field, adj_row):
    channels = whole_field.shape[1]
    safe_rows = jnp.maximum(adj_row, 0)
    gathered = whole_field[safe_rows] * (adj_row >= 0).astype(whole_field.dtype)[:, None, None]
    gathered = gathered.reshape(27, channels, BE, BE, BE)
    return columns(padded_field(gathered), BE)

def convolve(whole_field, adjacency, weight):

    def one_block(adj_row):
        return jnp.dot(weight, block_columns(whole_field, adj_row), preferred_element_type=jnp.float32)
    return lax.map(one_block, adjacency)

def weight_grad(whole_field, adjacency, gradient):

    def one_step(carry_sum, scan_item):
        adj_row, grad_block = scan_item
        cols_now = block_columns(whole_field, adj_row)
        return (carry_sum + jnp.dot(grad_block, cols_now.T, preferred_element_type=jnp.float32), None)
    channels = whole_field.shape[1]
    start_sum = jnp.zeros((channels, 27 * channels), jnp.float32)
    result_sum, _ = lax.scan(one_step, start_sum, (adjacency, gradient))
    return result_sum

def flipped(weight):
    channels = weight.shape[0]
    turned = weight.reshape(channels, 27, channels)[:, ::-1, :]
    return jnp.transpose(turned, (2, 1, 0)).reshape(channels, 27 * channels)

def reference(feats, cotangent, occupancy, counts, adjacency, w_first, w_second):
    block_index = jnp.arange(BLOCKS, dtype=jnp.int32)
    live_slots = block_index % NB < counts[block_index // NB, 0]
    voxel_mask = ((occupancy != 0) & live_slots[:, None]).astype(jnp.float32)
    mask_half = voxel_mask.astype(jnp.bfloat16)
    mask_wide = voxel_mask[:, None, :]
    masked = feats * mask_half[:, None, :]
    pre_first = convolve(masked, adjacency, w_first)
    hidden = (jax.nn.silu(pre_first) * mask_wide).astype(jnp.bfloat16)
    pre_second = convolve(hidden, adjacency, w_second)
    out_feats = (masked.astype(jnp.float32) + pre_second * mask_wide).astype(jnp.bfloat16)
    grad_two = cotangent * mask_half[:, None, :]
    back_two = convolve(grad_two, adjacency, flipped(w_second))
    sigmoid_first = jax.nn.sigmoid(pre_first)
    grad_one = (back_two * mask_wide * sigmoid_first * (1.0 + pre_first * (1.0 - sigmoid_first))).astype(jnp.bfloat16)
    back_one = convolve(grad_one, adjacency, flipped(w_first))
    grad_feats = (mask_wide * (cotangent.astype(jnp.float32) + back_one)).astype(jnp.bfloat16)
    scaling = 1.0 / math.sqrt(BLOCKS * BE ** 3)
    grad_first = weight_grad(masked, adjacency, grad_one) * scaling
    grad_second = weight_grad(hidden, adjacency, grad_two) * scaling
    return (out_feats, grad_feats, grad_first, grad_second)
```

```python
import functools
import math

import jax
import jax.numpy as jnp
import numpy as np
from jax import lax
from jax.experimental import pallas as pl
from jax.experimental.pallas import tpu as pltpu
from jax.sharding import Mesh, PartitionSpec as P

C = 96
BE = 8
GRID = 8
REPS = 8
ROWS = 208
PAD = 12
LANES = 1920
OUTER = 1536
INNER = 1152
BASE = PAD * PAD + PAD
TILES_R, TILES_L = 24, 21
DIRECTIONS = [(-1, -1), (0, -1), (1, -1), (-1, 0), (1, 0), (-1, 1), (0, 1), (1, 1)]
CORNERS = [(-1, -1), (1, -1), (-1, 1), (1, 1)]
OFFSETS = [(a, b, c) for a in (-1, 0, 1) for b in (-1, 0, 1) for c in (-1, 0, 1)]
F32, BF16 = jnp.float32, jnp.bfloat16


def pack_matrix():
    picks = np.zeros((512, 384), np.float32)
    for half, first in ((0, 6), (1, 0)):
        for x in range(8):
            for y in range(2):
                for z in range(8):
                    picks[x * 64 + (first + y) * 8 + z, half * 128 + x * 16 + y * 8 + z] = 1
    for number, (sx, sy) in enumerate(CORNERS):
        for x in range(2):
            for y in range(2):
                for z in range(8):
                    row = (x + (6 if sx < 0 else 0)) * 64 + (y + (6 if sy < 0 else 0)) * 8 + z
                    picks[row, 256 + 32 * number + x * 16 + y * 8 + z] = 1
    return picks


def place_table():
    table = np.full((16, LANES), -1, np.int32)
    table[0] = 27
    for p in range(PAD**3):
        at = (p // (PAD * PAD) - 2, p // PAD % PAD - 2, p % PAD - 2)
        site = [(-1 if a < 0 else 1 if a >= BE else 0) for a in at]
        x, y, z = (a % BE for a in at)
        table[0, p] = (site[0] + 1) * 9 + (site[1] + 1) * 3 + site[2] + 1
        table[1, p] = x * 64 + y * 8 + z
        for number, (sx, sy) in enumerate(DIRECTIONS):
            nx = x - 6 if sx < 0 else x
            ny = y - 6 if sy < 0 else y
            if sx != 0 and not 0 <= nx < 2 or sy != 0 and not 0 <= ny < 2:
                continue
            if sy == 0:
                place = 512 + nx * 64 + y * 8 + z
            elif sx == 0:
                place = 640 + x * 16 + ny * 8 + z
            else:
                place = 768 + 32 * CORNERS.index((sx, sy)) + nx * 16 + ny * 8 + z
            table[2 + number, p] = place
    return table


def inner_table():
    marks = np.zeros((8, OUTER), np.float32)
    squeeze = np.zeros((INNER, 512), np.float32)
    for x in range(8):
        for y in range(8):
            for z in range(8):
                t = x * PAD * PAD + y * PAD + z
                marks[0, t + BASE + 1] = 1
                marks[1, t] = 1
                squeeze[t, x * 64 + y * 8 + z] = 1
    return marks, squeeze


def pack_kernel(feats, cot, occ, picks, field, *sends):
    mask = (occ[...] != 0).astype(F32).astype(BF16)
    field[0:C, :] = feats[0] * mask
    field[C : 2 * C, :] = cot[0] * mask
    field[2 * C :, :] = jnp.broadcast_to(mask, (ROWS - 2 * C, 512))
    whole = field[...]
    rims = jnp.dot(whole, picks[...], preferred_element_type=F32).astype(BF16)
    left, right, down, up, corners = sends
    left[...] = whole[:, 384:512]
    right[...] = whole[:, 0:128]
    down[...] = rims[:, 0:128]
    up[...] = rims[:, 128:256]
    corners[...] = rims[:, 256:384]


def shifted_columns(source, columns, length):
    for number in range(9):
        start = (number // 3) * PAD * PAD + (number % 3) * PAD
        columns[number * C : (number + 1) * C, 0:length] = source[:, start : start + length]


def three_taps(weight, columns, length):
    parts = jnp.dot(weight[...], columns[:, 0:length], preferred_element_type=F32)
    return (
        parts[0:C]
        + pltpu.roll(parts[C : 2 * C], length - 1, 1)
        + pltpu.roll(parts[2 * C :], length - 2, 1)
    )


def weight_grad(gradient, columns, length, out, first_row):
    wide = gradient.astype(F32)
    stack = jnp.concatenate(
        [wide, pltpu.roll(wide, 1, 1), pltpu.roll(wide, 2, 1)], axis=0
    ).astype(BF16)
    sums = lax.dot_general(
        stack, columns[:, 0:length], (((1,), (1,)), ((), ())), preferred_element_type=F32
    ) * (1.0 / 512.0)
    for number in range(9):
        for dz in range(3):
            k = number * 3 + dz
            out[first_row : first_row + C, k * C : (k + 1) * C] = sums[
                dz * C : (dz + 1) * C, number * C : (number + 1) * C
            ]


def main_kernel(
    adj, own, field, xm, xp, ym, yp, c0, c1, c2, c3, table, marks, w_one, w_two,
    chunks, padded, hidden, grad_one,
    sources, col_m, col_g, grads,
):
    me = own[0]
    steps = [sx + GRID * sy for sx, sy in DIRECTIONS]
    numbers = []
    for k in range(27):
        block = adj[0, k]
        relative = block // REPS - me
        number = jnp.where(relative == 0, 1, -1)
        for d, step in enumerate(steps):
            number = jnp.where(relative == step, d + 2, number)
        numbers.append(jnp.where(block < 0, -1, number))

    def some(d):
        found = numbers[0] == d + 2
        for number in numbers[1:]:
            found = jnp.logical_or(found, number == d + 2)
        return found

    sources[:, 0:512] = field[...]

    @pl.when(some(3))
    def _():
        sources[:, 512:640] = xm[...]

    @pl.when(jnp.logical_not(some(3)))
    def _():
        sources[:, 512:640] = xp[...]

    @pl.when(some(1))
    def _():
        sources[:, 640:768] = ym[...]

    @pl.when(jnp.logical_not(some(1)))
    def _():
        sources[:, 640:768] = yp[...]

    sources[:, 768:896] = c0[...]
    for ref, d in ((c1, 2), (c2, 5), (c3, 7)):

        @pl.when(some(d))
        def _():
            sources[:, 768:896] = ref[...]

    site = table[0:1, :]
    which = jnp.full((1, LANES), -1, jnp.int32)
    for k in range(27):
        which = jnp.where(site == k, numbers[k], which)
    place = jnp.full((1, LANES), -1, jnp.int32)
    for d in range(9):
        place = jnp.where(which == d + 1, table[d + 1 : d + 2, :], place)

    width = 384
    for part in range(LANES // width):
        cut = slice(part * width, (part + 1) * width)
        rows = lax.broadcasted_iota(jnp.int32, (896, width), 0)
        hot = jnp.where(rows == place[:, cut], 1.0, 0.0).astype(BF16)
        padded[:, cut] = jnp.dot(sources[...], hot, preferred_element_type=F32).astype(BF16)

    shifted_columns(padded[0:C, :], col_m, OUTER)
    shifted_columns(padded[C : 2 * C, :], col_g, OUTER)
    mask = padded[2 * C : 2 * C + 1, BASE + 1 : BASE + 1 + OUTER].astype(F32)
    pre = three_taps(w_one, col_m, OUTER)
    sig = jax.nn.sigmoid(pre)
    hidden[...] = (pre * sig * mask).astype(BF16)
    back = three_taps(w_two, col_g, OUTER)
    grad = (back * mask * sig * (1.0 + pre * (1.0 - sig))).astype(BF16)
    grad_one[...] = grad
    grads[:, 27 * C :] = jnp.zeros((2 * C, TILES_L * 128 - 27 * C), F32)
    weight_grad(grad.astype(F32) * marks[0:1, :], col_m, OUTER, grads, 0)
    shifted_columns(hidden[...], col_g, INNER)
    start = 2 * (BASE + 1)
    grad_two = padded[C : 2 * C, start : start + INNER].astype(F32) * marks[1:2, 0:INNER]
    weight_grad(grad_two, col_g, INNER, grads, C)
    for row in range(TILES_R):
        for lane in range(TILES_L):
            chunks[row * TILES_L + lane] = grads[
                row * 8 : (row + 1) * 8, lane * 128 : (lane + 1) * 128
            ]
    chunks[TILES_R * TILES_L :] = jnp.zeros((8, 8, 128), F32)


def out_kernel(padded, hidden, grad_one, squeeze, w_two, w_one, out_feats, grad_feats, columns):
    start = 2 * (BASE + 1)
    mask = padded[2 * C : 2 * C + 1, start : start + INNER].astype(F32)
    for first, field, weight, out in (
        (0, hidden, w_two, out_feats),
        (C, grad_one, w_one, grad_feats),
    ):
        shifted_columns(field[...], columns, INNER)
        pre = three_taps(weight, columns, INNER)
        kept = padded[first : first + C, start : start + INNER].astype(F32)
        wide = (kept + pre * mask).astype(BF16)
        out[0] = jnp.dot(wide, squeeze[...], preferred_element_type=F32).astype(BF16)


def unpack_kernel(chunks, first, second):
    for row in range(TILES_R):
        out = first if row < 12 else second
        rows = slice(row % 12 * 8, row % 12 * 8 + 8)
        for lane in range(TILES_L):
            last = min((lane + 1) * 128, 27 * C)
            out[rows, lane * 128 : last] = chunks[row * TILES_L + lane][:, : last - lane * 128]


def forward_weight(weight):
    taps = weight.reshape(C, 9, 3, C)
    return jnp.transpose(taps, (2, 0, 1, 3)).reshape(3 * C, 9 * C)


def turned_weight(weight):
    taps = weight.reshape(C, 27, C)[:, ::-1, :].reshape(C, 9, 3, C)
    return jnp.transpose(taps, (2, 3, 1, 0)).reshape(3 * C, 9 * C)


VMEM = pl.BlockSpec(memory_space=pltpu.VMEM)
SMEM = pl.BlockSpec(memory_space=pltpu.SMEM)
PARAMS = pltpu.CompilerParams(vmem_limit_bytes=48 * 1024 * 1024)


def shape(dims, dtype):
    return jax.ShapeDtypeStruct(dims, dtype)


def body(feats, cotangent, occupancy, counts, adjacency, w_first, w_second):
    own = lax.axis_index("space")
    rim = shape((ROWS, 128), BF16)
    marks, squeeze = inner_table()
    with jax.named_scope("pack"):
        field, left, right, down, up, corners = pl.pallas_call(
            pack_kernel,
            out_shape=[shape((ROWS, 512), BF16)] + [rim] * 5,
            in_specs=[VMEM] * 4,
            out_specs=[VMEM] * 6,
            compiler_params=PARAMS,
        )(feats, cotangent, occupancy, jnp.asarray(pack_matrix(), BF16))
    sent = {(-1, 0): left, (1, 0): right, (0, -1): down, (0, 1): up}
    near = []
    with jax.named_scope("rims"):
        for sx, sy in DIRECTIONS:
            step = sx + GRID * sy
            pairs = []
            for owner in range(GRID * GRID):
                column, row = owner % GRID + sx, owner // GRID + sy
                if 0 <= column < GRID and 0 <= row < GRID:
                    pairs.append((owner + step, owner))
            near.append(lax.ppermute(sent.get((sx, sy), corners), "space", pairs))
    c0, ym, c1, xm, xp, c2, yp, c3 = near
    one_f, one_b = forward_weight(w_first), turned_weight(w_first)
    two_f, two_b = forward_weight(w_second), turned_weight(w_second)
    with jax.named_scope("middle"):
        chunks, padded, hidden, grad_one = pl.pallas_call(
            main_kernel,
            out_shape=[
                shape((512, 8, 128), F32),
                shape((ROWS, LANES), BF16),
                shape((C, OUTER), BF16),
                shape((C, OUTER), BF16),
            ],
            in_specs=[SMEM, SMEM] + [VMEM] * 13,
            out_specs=[VMEM] * 4,
            scratch_shapes=[
                pltpu.VMEM((ROWS, 896), BF16),
                pltpu.VMEM((9 * C, OUTER), BF16),
                pltpu.VMEM((9 * C, OUTER), BF16),
                pltpu.VMEM((2 * C, TILES_L * 128), F32),
            ],
            compiler_params=PARAMS,
        )(
            adjacency, own.reshape(1), field, xm, xp, ym, yp, c0, c1, c2, c3,
            jnp.asarray(place_table()), jnp.asarray(marks), one_f, two_b,
        )
    with jax.named_scope("sum"):
        total = lax.psum(chunks, ("space", "rep"))
    with jax.named_scope("outputs"):
        out_feats, grad_feats = pl.pallas_call(
            out_kernel,
            out_shape=[shape((1, C, 512), BF16)] * 2,
            in_specs=[VMEM] * 6,
            out_specs=[VMEM] * 2,
            scratch_shapes=[pltpu.VMEM((9 * C, INNER), BF16)],
            compiler_params=PARAMS,
        )(padded, hidden, grad_one, jnp.asarray(squeeze, BF16), two_f, one_b)
    with jax.named_scope("unpack"):
        grad_first, grad_second = pl.pallas_call(
            unpack_kernel,
            out_shape=[shape((C, 27 * C), F32)] * 2,
            in_specs=[VMEM],
            out_specs=[VMEM] * 2,
            compiler_params=PARAMS,
        )(total)
    return out_feats, grad_feats, grad_first, grad_second


def solution(mesh):
    both = ("space", "rep")
    blocks = P(both, None, None)
    rows = P(both, None)
    return jax.shard_map(
        body,
        mesh=mesh,
        in_specs=(blocks, blocks, rows, rows, rows, P(), P()),
        out_specs=(blocks, blocks, P(), P()),
        check_vma=False,
    )
```

```python
import jax
import jax.numpy as jnp
import numpy as np
from jax import lax
from jax.experimental import pallas as pl
from jax.experimental.pallas import tpu as pltpu
from jax.sharding import Mesh, PartitionSpec as P

C = 96
BE = 8
GRID = 8
REPS = 8
ROWS = 208
PAD = 12
LANES = 1920
OUTER = 1536
INNER = 1152
BASE = PAD * PAD + PAD
TILES_L = 21
DIRECTIONS = [(-1, -1), (0, -1), (1, -1), (-1, 0), (1, 0), (-1, 1), (0, 1), (1, 1)]
OFFSETS = [(a, b, c) for a in (-1, 0, 1) for b in (-1, 0, 1) for c in (-1, 0, 1)]
F32, BF16 = jnp.float32, jnp.bfloat16


def rim_matrix():
    picks = np.zeros((768, 512), np.float32)
    for half, first in ((0, 6), (1, 0)):
        for y in range(2):
            for z in range(8):
                for x in range(8):
                    picks[x * 64 + (first + y) * 8 + z, half * 256 + x * 16 + y * 8 + z] = 1
                for x in range(2):
                    rim = x * 64 + (first + y) * 8 + z
                    picks[512 + rim, half * 256 + 128 + x * 16 + y * 8 + z] = 1
                    picks[640 + rim, half * 256 + 160 + x * 16 + y * 8 + z] = 1
    return picks


def place_table():
    table = np.full((16, LANES), -1, np.int32)
    table[0] = 27
    for p in range(PAD**3):
        at = (p // (PAD * PAD) - 2, p // PAD % PAD - 2, p % PAD - 2)
        site = [(-1 if a < 0 else 1 if a >= BE else 0) for a in at]
        x, y, z = (a % BE for a in at)
        table[0, p] = (site[0] + 1) * 9 + (site[1] + 1) * 3 + site[2] + 1
        table[1, p] = x * 64 + y * 8 + z
        for number, (sx, sy) in enumerate(DIRECTIONS):
            nx = x - 6 if sx < 0 else x
            ny = y - 6 if sy < 0 else y
            if sx != 0 and not 0 <= nx < 2 or sy != 0 and not 0 <= ny < 2:
                continue
            if sy == 0:
                place = 512 + nx * 64 + y * 8 + z
            elif sx == 0:
                place = 640 + x * 16 + ny * 8 + z
            else:
                place = (768 if sx < 0 else 800) + nx * 16 + ny * 8 + z
            table[2 + number, p] = place
    return table


def inner_table():
    marks = np.zeros((8, OUTER), np.float32)
    squeeze = np.zeros((INNER, 512), np.float32)
    for x in range(8):
        for y in range(8):
            for z in range(8):
                t = x * PAD * PAD + y * PAD + z
                marks[0, t + BASE + 1] = 1
                marks[1, t] = 1
                squeeze[t, x * 64 + y * 8 + z] = 1
    return marks, squeeze


def pack_kernel(feats_in, cot_in, occ_in, field, left, right, feats, cot, occ, sems):
    copies = [
        pltpu.make_async_copy(source, target, sems.at[number])
        for number, (source, target) in enumerate(((occ_in, occ), (feats_in, feats), (cot_in, cot)))
    ]
    for copy in copies:
        copy.start()
    copies[0].wait()
    mask = (occ[...] != 0).astype(F32).astype(BF16)
    field[2 * C :, :] = jnp.broadcast_to(mask, (ROWS - 2 * C, 512))
    copies[1].wait()
    field[0:C, :] = feats[0] * mask
    copies[2].wait()
    field[C : 2 * C, :] = cot[0] * mask
    left[...] = field[:, 384:512]
    right[...] = field[:, 0:128]


def rim_kernel(field, xm, xp, picks, down, up):
    sources = jnp.concatenate([field[...], xm[...], xp[...]], axis=1)
    rims = jnp.dot(sources, picks[...], preferred_element_type=F32).astype(BF16)
    down[...] = rims[:, 0:256]
    up[...] = rims[:, 256:512]


def weight_kernel(first, second, first_forward, first_turned, second_forward, second_turned):
    for weight, forward, turned in (
        (first, first_forward, first_turned),
        (second, second_forward, second_turned),
    ):
        whole = weight[...]
        across = whole.astype(F32).T.astype(BF16)
        for number in range(9):
            for dz in range(3):
                k = number * 3 + dz
                rows = slice(dz * C, (dz + 1) * C)
                columns = slice(number * C, (number + 1) * C)
                forward[rows, columns] = whole[:, k * C : (k + 1) * C]
                turned[rows, columns] = across[(26 - k) * C : (27 - k) * C, :]


def shifted_columns(source, columns, length):
    for number in range(9):
        start = (number // 3) * PAD * PAD + (number % 3) * PAD
        columns[number * C : (number + 1) * C, 0:length] = source[:, start : start + length]


def three_taps(weight, columns, length):
    parts = jnp.dot(weight[...], columns[:, 0:length], preferred_element_type=F32)
    return (
        parts[0:C]
        + pltpu.roll(parts[C : 2 * C], length - 1, 1)
        + pltpu.roll(parts[2 * C :], length - 2, 1)
    )


def weight_grad(gradient, columns, length, out, first_row):
    wide = gradient.astype(F32)
    stack = jnp.concatenate(
        [wide, pltpu.roll(wide, 1, 1), pltpu.roll(wide, 2, 1)], axis=0
    ).astype(BF16)
    sums = lax.dot_general(
        stack, columns[:, 0:length], (((1,), (1,)), ((), ())), preferred_element_type=F32
    ) * (1.0 / 512.0)
    for number in range(9):
        for dz in range(3):
            k = number * 3 + dz
            out[first_row : first_row + C, k * C : (k + 1) * C] = sums[
                dz * C : (dz + 1) * C, number * C : (number + 1) * C
            ]


def main_kernel(
    adj, own, field, xm, xp, ym, yp, table, marks, w_one, w_two,
    keep, send, padded, hidden, grad_one,
    sources, col_m, col_g, grads,
):
    me = own[0]
    steps = [sx + GRID * sy for sx, sy in DIRECTIONS]
    numbers = []
    for k in range(27):
        block = adj[0, k]
        relative = block // REPS - me
        number = jnp.where(relative == 0, 1, -1)
        for d, step in enumerate(steps):
            number = jnp.where(relative == step, d + 2, number)
        numbers.append(jnp.where(block < 0, -1, number))

    def some(*directions):
        found = numbers[0] == directions[0] + 2
        for number in numbers:
            for d in directions:
                found = jnp.logical_or(found, number == d + 2)
        return found

    sources[:, 0:512] = field[...]
    at_left, at_low = some(3), some(0, 1, 2)

    @pl.when(at_left)
    def _():
        sources[:, 512:640] = xm[...]

    @pl.when(jnp.logical_not(at_left))
    def _():
        sources[:, 512:640] = xp[...]

    @pl.when(at_low)
    def _():
        sources[:, 640:896] = ym[...]

    @pl.when(jnp.logical_not(at_low))
    def _():
        sources[:, 640:896] = yp[...]

    site = table[0:1, :]
    which = jnp.full((1, LANES), -1, jnp.int32)
    for k in range(27):
        which = jnp.where(site == k, numbers[k], which)
    place = jnp.full((1, LANES), -1, jnp.int32)
    for d in range(9):
        place = jnp.where(which == d + 1, table[d + 1 : d + 2, :], place)

    width = 384
    for part in range(LANES // width):
        cut = slice(part * width, (part + 1) * width)
        rows = lax.broadcasted_iota(jnp.int32, (896, width), 0)
        hot = jnp.where(rows == place[:, cut], 1.0, 0.0).astype(BF16)
        padded[:, cut] = jnp.dot(sources[...], hot, preferred_element_type=F32).astype(BF16)

    shifted_columns(padded[0:C, :], col_m, OUTER)
    shifted_columns(padded[C : 2 * C, :], col_g, OUTER)
    mask = padded[2 * C : 2 * C + 1, BASE + 1 : BASE + 1 + OUTER].astype(F32)
    pre = three_taps(w_one, col_m, OUTER)
    sig = jax.nn.sigmoid(pre)
    hidden[...] = (pre * sig * mask).astype(BF16)
    back = three_taps(w_two, col_g, OUTER)
    grad = (back * mask * sig * (1.0 + pre * (1.0 - sig))).astype(BF16)
    grad_one[...] = grad
    grads[:, 27 * C :] = jnp.zeros((2 * C, TILES_L * 128 - 27 * C), F32)
    weight_grad(grad.astype(F32) * marks[0:1, :], col_m, OUTER, grads, 0)
    shifted_columns(hidden[...], col_g, INNER)
    start = 2 * (BASE + 1)
    grad_two = padded[C : 2 * C, start : start + INNER].astype(F32) * marks[1:2, 0:INNER]
    weight_grad(grad_two, col_g, INNER, grads, C)

    def split(halves):
        for tile in range(256):
            half, place = halves[tile // 128], tile % 128
            if tile < 12 * TILES_L:
                row, lane = tile // TILES_L * 16, tile % TILES_L * 128
                half[place] = grads[row : row + 16, lane : lane + 128]
            else:
                half[place] = jnp.zeros((16, 128), F32)

    @pl.when(own[1] == 0)
    def _():
        split((keep, send))

    @pl.when(own[1] != 0)
    def _():
        split((send, keep))


def out_kernel(padded, hidden, grad_one, squeeze, w_two, w_one, out_feats, grad_feats, columns):
    start = 2 * (BASE + 1)
    mask = padded[2 * C : 2 * C + 1, start : start + INNER].astype(F32)
    for first, field, weight, out in (
        (0, hidden, w_two, out_feats),
        (C, grad_one, w_one, grad_feats),
    ):
        shifted_columns(field[...], columns, INNER)
        pre = three_taps(weight, columns, INNER)
        kept = padded[first : first + C, start : start + INNER].astype(F32)
        wide = (kept + pre * mask).astype(BF16)
        out[0] = jnp.dot(wide, squeeze[...], preferred_element_type=F32).astype(BF16)


def unpack_kernel(own, mine, other, first, second):
    def join(halves):
        for tile in range(12 * TILES_L):
            row, lane = tile // TILES_L * 16, tile % TILES_L * 128
            out = first if row < C else second
            last = min(lane + 128, 27 * C)
            part = halves[tile // 128][tile % 128].astype(F32)
            out[row % C : row % C + 16, lane:last] = part[:, : last - lane]

    @pl.when(own[1] == 0)
    def _():
        join((mine, other))

    @pl.when(own[1] != 0)
    def _():
        join((other, mine))


VMEM = pl.BlockSpec(memory_space=pltpu.VMEM)
SMEM = pl.BlockSpec(memory_space=pltpu.SMEM)
PARAMS = pltpu.CompilerParams(vmem_limit_bytes=48 * 1024 * 1024)


def shape(dims, dtype):
    return jax.ShapeDtypeStruct(dims, dtype)


def call(kernel, outs, specs, scratch=()):
    return pl.pallas_call(
        kernel,
        out_shape=[shape(*out) for out in outs],
        in_specs=specs,
        out_specs=[VMEM] * len(outs),
        scratch_shapes=scratch,
        compiler_params=PARAMS,
    )


def from_owner(value, sx, sy):
    pairs = []
    for owner in range(GRID * GRID):
        column, row = owner % GRID + sx, owner // GRID + sy
        if 0 <= column < GRID and 0 <= row < GRID:
            pairs.append((row * GRID + column, owner))
    return lax.ppermute(value, ("z", "y"), pairs)


def sum_shares(value, axes, count):
    parts = lax.all_to_all(value, axes, 0, 0, tiled=True)
    parts = parts.reshape((count, value.shape[0] // count) + value.shape[1:])
    return jnp.sum(parts.astype(F32), axis=0)


def all_shares(value, axes, count):
    copies = jnp.broadcast_to(value[None], (count,) + value.shape)
    return lax.all_to_all(copies, axes, 0, 0).reshape((count * value.shape[0],) + value.shape[1:])


def body(feats, cotangent, occupancy, counts, adjacency, w_first, w_second):
    own = jnp.stack([lax.axis_index(("z", "y")), lax.axis_index("core")]).astype(jnp.int32)
    marks, squeeze = inner_table()
    wide, rim, turned = ((ROWS, 512), BF16), ((ROWS, 128), BF16), ((3 * C, 9 * C), BF16)
    with jax.named_scope("pack"):
        field, left, right = call(
            pack_kernel,
            [wide, rim, rim],
            [pl.BlockSpec(memory_space=pl.ANY)] * 3,
            [
                pltpu.VMEM((1, C, 512), BF16),
                pltpu.VMEM((1, C, 512), BF16),
                pltpu.VMEM((1, 512), jnp.int32),
                pltpu.SemaphoreType.DMA((3,)),
            ],
        )(feats, cotangent, occupancy)
    with jax.named_scope("weights"):
        one_f, one_b, two_f, two_b = call(weight_kernel, [turned] * 4, [VMEM] * 2)(w_first, w_second)
    with jax.named_scope("rims_x"):
        xm, xp = from_owner(left, -1, 0), from_owner(right, 1, 0)
    with jax.named_scope("rim_rows"):
        down, up = call(rim_kernel, [((ROWS, 256), BF16)] * 2, [VMEM] * 4)(
            field, xm, xp, jnp.asarray(rim_matrix(), BF16)
        )
    with jax.named_scope("rims_y"):
        ym, yp = from_owner(down, 0, -1), from_owner(up, 0, 1)
    half = ((128, 16, 128), F32)
    with jax.named_scope("middle"):
        keep, send, padded, hidden, grad_one = call(
            main_kernel,
            [half, half, ((ROWS, LANES), BF16), ((C, OUTER), BF16), ((C, OUTER), BF16)],
            [SMEM, SMEM] + [VMEM] * 9,
            [
                pltpu.VMEM((ROWS, 896), BF16),
                pltpu.VMEM((9 * C, OUTER), BF16),
                pltpu.VMEM((9 * C, OUTER), BF16),
                pltpu.VMEM((2 * C, TILES_L * 128), F32),
            ],
        )(
            adjacency, own, field, xm, xp, ym, yp,
            jnp.asarray(place_table()), jnp.asarray(marks), one_f, two_b,
        )
    with jax.named_scope("sum"):
        swap = [(0, 1), (1, 0)]
        pair = (keep + lax.ppermute(send, "core", swap)).astype(BF16)
        plane = sum_shares(pair, ("y", "x"), 16)
        total = sum_shares(plane.reshape(16, 8, 128), "z", 16)
        total = all_shares(total.astype(BF16), "z", 16)
        mine = all_shares(total.reshape(8, 16, 128), ("y", "x"), 16)
        other = lax.ppermute(mine, "core", swap)
    with jax.named_scope("outputs"):
        out_feats, grad_feats = call(
            out_kernel,
            [((1, C, 512), BF16)] * 2,
            [VMEM] * 6,
            [pltpu.VMEM((9 * C, INNER), BF16)],
        )(padded, hidden, grad_one, jnp.asarray(squeeze, BF16), two_f, one_b)
    with jax.named_scope("unpack"):
        grad_first, grad_second = call(
            unpack_kernel, [((C, 27 * C), F32)] * 2, [SMEM] + [VMEM] * 2
        )(own, mine, other)
    return out_feats, grad_feats, grad_first, grad_second


def solution(mesh):
    fine = Mesh(mesh.devices.reshape(16, 4, 4, 2), ("z", "y", "x", "core"))
    both = ("z", "y", "x", "core")
    blocks = P(both, None, None)
    rows = P(both, None)
    return jax.shard_map(
        body,
        mesh=fine,
        in_specs=(blocks, blocks, rows, rows, rows, P(), P()),
        out_specs=(blocks, blocks, P(), P()),
        check_vma=False,
    )
```

```python
import jax
import jax.numpy as jnp
import numpy as np
from jax import lax
from jax.experimental import pallas as pl
from jax.experimental.pallas import tpu as pltpu
from jax.sharding import Mesh, PartitionSpec as P

C = 96
BE = 8
GRID = 8
REPS = 8
ROWS = 208
PAD = 12
LANES = 1920
OUTER = 1536
INNER = 1152
BASE = PAD * PAD + PAD
TILES_L = 21
DIRECTIONS = [(-1, -1), (0, -1), (1, -1), (-1, 0), (1, 0), (-1, 1), (0, 1), (1, 1)]
OFFSETS = [(a, b, c) for a in (-1, 0, 1) for b in (-1, 0, 1) for c in (-1, 0, 1)]
F32, BF16 = jnp.float32, jnp.bfloat16


def place_table():
    table = np.full((16, LANES), -1, np.int32)
    table[0] = 27
    for p in range(PAD**3):
        at = (p // (PAD * PAD) - 2, p // PAD % PAD - 2, p % PAD - 2)
        site = [(-1 if a < 0 else 1 if a >= BE else 0) for a in at]
        x, y, z = (a % BE for a in at)
        table[0, p] = (site[0] + 1) * 9 + (site[1] + 1) * 3 + site[2] + 1
        table[1, p] = x * 64 + y * 8 + z
        for number, (sx, sy) in enumerate(DIRECTIONS):
            nx = x - 6 if sx < 0 else x
            ny = y - 6 if sy < 0 else y
            if sx != 0 and not 0 <= nx < 2 or sy != 0 and not 0 <= ny < 2:
                continue
            if sx == 0:
                place = 512 + x * 16 + ny * 8 + z
            elif sy == 0:
                place = 640 + nx * 64 + y * 8 + z
            else:
                place = (768 if sy < 0 else 800) + nx * 16 + ny * 8 + z
            table[2 + number, p] = place
    return table


def ints(dims, axis):
    return lax.broadcasted_iota(jnp.int32, dims, axis)


def pack_kernel(feats_in, cot_in, occ_in, field, down, up, feats, cot, occ, sems):
    copies = [
        pltpu.make_async_copy(source, target, sems.at[number])
        for number, (source, target) in enumerate(((occ_in, occ), (feats_in, feats), (cot_in, cot)))
    ]
    for copy in copies:
        copy.start()
    lane = ints((512, 256), 1)
    rim = lane % 128
    wanted = rim // 16 * 64 + rim // 8 % 2 * 8 + rim % 8 + jnp.where(lane < 128, 48, 0)
    picks = jnp.where(ints((512, 256), 0) == wanted, 1.0, 0.0).astype(BF16)
    copies[0].wait()
    mask = (occ[...] != 0).astype(F32).astype(BF16)
    field[2 * C :, :] = jnp.broadcast_to(mask, (ROWS - 2 * C, 512))
    copies[1].wait()
    field[0:C, :] = feats[0] * mask
    copies[2].wait()
    field[C : 2 * C, :] = cot[0] * mask
    rims = jnp.dot(field[...], picks, preferred_element_type=F32).astype(BF16)
    down[...] = rims[:, 0:128]
    up[...] = rims[:, 128:256]


def slab_kernel(field, ym, yp, left, right):
    blank = jnp.zeros((ROWS, 64), BF16)
    left[:, 0:128] = field[:, 384:512]
    left[:, 128:256] = jnp.concatenate([ym[:, 96:128], yp[:, 96:128], blank], axis=1)
    right[:, 0:128] = field[:, 0:128]
    right[:, 128:256] = jnp.concatenate([ym[:, 0:32], yp[:, 0:32], blank], axis=1)


def weight_kernel(
    first_in, second_in, first_forward, first_turned, second_forward, second_turned,
    first, second, sems,
):
    copies = [
        pltpu.make_async_copy(first_in, first, sems.at[0]),
        pltpu.make_async_copy(second_in, second, sems.at[1]),
    ]
    for copy in copies:
        copy.start()
    for copy, weight, forward, turned in (
        (copies[0], first, first_forward, first_turned),
        (copies[1], second, second_forward, second_turned),
    ):
        copy.wait()
        whole = weight[...]
        across = whole.astype(F32).T.astype(BF16)
        for number in range(9):
            for dz in range(3):
                k = number * 3 + dz
                rows = slice(dz * C, (dz + 1) * C)
                columns = slice(number * C, (number + 1) * C)
                forward[rows, columns] = whole[:, k * C : (k + 1) * C]
                turned[rows, columns] = across[(26 - k) * C : (27 - k) * C, :]


def shifted_columns(source, columns, length):
    for number in range(9):
        start = (number // 3) * PAD * PAD + (number % 3) * PAD
        columns[number * C : (number + 1) * C, 0:length] = source[:, start : start + length]


def three_taps(weight, columns, length):
    parts = jnp.dot(weight[...], columns[:, 0:length], preferred_element_type=F32)
    return (
        parts[0:C]
        + pltpu.roll(parts[C : 2 * C], length - 1, 1)
        + pltpu.roll(parts[2 * C :], length - 2, 1)
    )


def weight_grad(gradient, columns, length, grads, tiles):
    stack = jnp.concatenate(
        [gradient, pltpu.roll(gradient, 1, 1), pltpu.roll(gradient, 2, 1)], axis=0
    ).astype(BF16)
    sums = lax.dot_general(
        stack, columns[:, 0:length], (((1,), (1,)), ((), ())), preferred_element_type=F32
    ) * (1.0 / 512.0)
    for number in range(9):
        for dz in range(3):
            k = number * 3 + dz
            grads[:, k * C : (k + 1) * C] = sums[
                dz * C : (dz + 1) * C, number * C : (number + 1) * C
            ]
    grads[:, 27 * C :] = jnp.zeros((C, TILES_L * 128 - 27 * C), F32)
    for tile in range(6 * TILES_L):
        row, lane = tile // TILES_L * 16, tile % TILES_L * 128
        tiles[tile] = grads[row : row + 16, lane : lane + 128]
    tiles[6 * TILES_L :] = jnp.zeros((128 - 6 * TILES_L, 16, 128), F32)


def first_grad(padded, grad_one, table, columns, grads, tiles):
    own = table[0:1, BASE + 1 : BASE + 1 + OUTER] == 13
    weight_grad(jnp.where(own, grad_one[...].astype(F32), 0.0), columns, OUTER, grads, tiles)


def second_grad(padded, grad_one, table, columns, grads, tiles):
    start = 2 * (BASE + 1)
    own = table[0:1, start : start + INNER] == 13
    grad_two = padded[C : 2 * C, start : start + INNER].astype(F32)
    weight_grad(jnp.where(own, grad_two, 0.0), columns, INNER, grads, tiles)


def relative_owners(adj, own):
    owners = [adj[0, k] for k in range(27)]
    return [jnp.where(block < 0, 99, block // REPS - own[0]) for block in owners]


def among(relative, steps):
    found = relative[0] == steps[0]
    for value in relative:
        for step in steps:
            found = jnp.logical_or(found, value == step)
    return found


def place_kernel(adj, own, field, ym, yp, table, base, hot_x, sources):
    relative = relative_owners(adj, own)
    from_low = among(relative, [-GRID])
    sources[:, 0:512] = field[...]

    @pl.when(from_low)
    def _():
        sources[:, 512:640] = ym[...]

    @pl.when(jnp.logical_not(from_low))
    def _():
        sources[:, 512:640] = yp[...]

    site = table[0:1, :]
    which = jnp.full((1, LANES), 99, jnp.int32)
    for k in range(27):
        which = jnp.where(site == k, relative[k], which)
    place = jnp.where(which == 0, table[1:2, :], -1)
    for number, (sx, sy) in enumerate(DIRECTIONS):
        place = jnp.where(which == sx + GRID * sy, table[number + 2 : number + 3, :], place)
    width = 384
    for part in range(LANES // width):
        cut = slice(part * width, (part + 1) * width)
        hot = jnp.where(ints((896, width), 0) == place[:, cut], 1.0, 0.0).astype(BF16)
        hot_x[:, cut] = hot[640:896]
        base[:, cut] = jnp.dot(
            sources[...], hot[0:640], preferred_element_type=F32
        ).astype(BF16)


def main_kernel(
    adj, own, xm, xp, base, hot_x, table, w_one, w_two,
    send, padded, hidden, grad_one, col_m, col_h,
    slab, col_g, grads,
):
    from_left = among(relative_owners(adj, own), [-1 - GRID, -1, -1 + GRID])

    @pl.when(from_left)
    def _():
        slab[...] = xm[...]

    @pl.when(jnp.logical_not(from_left))
    def _():
        slab[...] = xp[...]

    width = 384
    for part in range(LANES // width):
        cut = slice(part * width, (part + 1) * width)
        near = jnp.dot(slab[...], hot_x[:, cut], preferred_element_type=F32)
        padded[:, cut] = (base[:, cut].astype(F32) + near).astype(BF16)
    shifted_columns(padded[0:C, :], col_m, OUTER)
    shifted_columns(padded[C : 2 * C, :], col_g, OUTER)
    mask = padded[2 * C : 2 * C + 1, BASE + 1 : BASE + 1 + OUTER].astype(F32)
    pre = three_taps(w_one, col_m, OUTER)
    sig = jax.nn.sigmoid(pre)
    hidden[...] = (pre * sig * mask).astype(BF16)
    back = three_taps(w_two, col_g, OUTER)
    grad_one[...] = (back * mask * sig * (1.0 + pre * (1.0 - sig))).astype(BF16)
    shifted_columns(hidden[...], col_h, INNER)

    @pl.when(own[1] == 0)
    def _():
        second_grad(padded, grad_one, table, col_h, grads, send)

    @pl.when(own[1] != 0)
    def _():
        first_grad(padded, grad_one, table, col_m, grads, send)


def keep_kernel(own, padded, grad_one, table, col_m, col_h, keep, grads):
    @pl.when(own[1] == 0)
    def _():
        first_grad(padded, grad_one, table, col_m, grads, keep)

    @pl.when(own[1] != 0)
    def _():
        second_grad(padded, grad_one, table, col_h, grads, keep)


def out_kernel(after, padded, hidden, grad_one, w_two, w_one, out_feats, grad_feats, done, columns):
    done[...] = jnp.zeros((8, 128), F32)
    voxel = ints((INNER, 512), 1)
    inner = voxel // 64 * (PAD * PAD) + voxel // 8 % 8 * PAD + voxel % 8
    squeeze = jnp.where(ints((INNER, 512), 0) == inner, 1.0, 0.0).astype(BF16)
    start = 2 * (BASE + 1)
    mask = padded[2 * C : 2 * C + 1, start : start + INNER].astype(F32)
    for first, field, weight, out in (
        (0, hidden, w_two, out_feats),
        (C, grad_one, w_one, grad_feats),
    ):
        shifted_columns(field[...], columns, INNER)
        pre = three_taps(weight, columns, INNER)
        kept = padded[first : first + C, start : start + INNER].astype(F32)
        wide = (kept + pre * mask).astype(BF16)
        out[0] = jnp.dot(wide, squeeze, preferred_element_type=F32).astype(BF16)


def share_kernel(count, parts, *refs):
    total = parts[0].astype(F32)
    for number in range(1, count):
        total = total + parts[number].astype(F32)
    copies = refs[-1]
    for number in range(copies.shape[0]):
        copies[number] = total.astype(BF16)


def write_half(half, out, rows, sems):
    copies = []
    for row in range(6):
        for lane in range(TILES_L):
            last = min((lane + 1) * 128, 27 * C)
            part = half[row * TILES_L + lane].astype(F32)
            rows[row * 16 : row * 16 + 16, lane * 128 : last] = part[:, : last - lane * 128]
        at = pl.ds(row * 16, 16)
        copies.append(pltpu.make_async_copy(rows.at[at], out.at[at], sems.at[row]))
        copies[-1].start()
    for copy in copies:
        copy.wait()


def mine_kernel(own, half, first, second, rows, sems):
    @pl.when(own[1] == 0)
    def _():
        write_half(half, first, rows, sems)

    @pl.when(own[1] != 0)
    def _():
        write_half(half, second, rows, sems)


def other_kernel(own, half, first_in, second_in, first, second, rows, sems):
    @pl.when(own[1] == 0)
    def _():
        write_half(half, second, rows, sems)

    @pl.when(own[1] != 0)
    def _():
        write_half(half, first, rows, sems)


VMEM = pl.BlockSpec(memory_space=pltpu.VMEM)
SMEM = pl.BlockSpec(memory_space=pltpu.SMEM)
HBM = pl.BlockSpec(memory_space=pltpu.HBM)
ANY = pl.BlockSpec(memory_space=pl.ANY)
DMA = pltpu.SemaphoreType.DMA
MIB = 1024 * 1024


def call(kernel, outs, specs, scratch=(), place=VMEM, limit=40 * MIB, **options):
    return pl.pallas_call(
        kernel,
        out_shape=[jax.ShapeDtypeStruct(*out) for out in outs],
        in_specs=specs,
        out_specs=[place] * len(outs),
        scratch_shapes=scratch,
        compiler_params=pltpu.CompilerParams(vmem_limit_bytes=limit),
        **options,
    )


def from_owner(value, sx, sy):
    pairs = []
    for owner in range(GRID * GRID):
        column, row = owner % GRID + sx, owner // GRID + sy
        if 0 <= column < GRID and 0 <= row < GRID:
            pairs.append((row * GRID + column, owner))
    return lax.ppermute(value, ("zh", "zl", "y"), pairs)


def swap_halves(value):
    return lax.ppermute(value, "core", [(0, 1), (1, 0)])


def body(feats, cotangent, occupancy, counts, adjacency, w_first, w_second):
    own = jnp.stack([lax.axis_index(("zh", "zl", "y")), lax.axis_index("core")]).astype(jnp.int32)
    table = jnp.asarray(place_table())
    rim, slab, turned = ((ROWS, 128), BF16), ((ROWS, 256), BF16), ((3 * C, 9 * C), BF16)
    vmem = pltpu.VMEM
    with jax.named_scope("pack"):
        field, down, up = call(
            pack_kernel,
            [((ROWS, 512), BF16), rim, rim],
            [HBM] * 3,
            [vmem((1, C, 512), BF16)] * 2 + [vmem((1, 512), jnp.int32), DMA((3,))],
        )(feats, cotangent, occupancy)
    with jax.named_scope("weights"):
        one_f, one_b, two_f, two_b = call(
            weight_kernel, [turned] * 4, [HBM] * 2, [vmem((C, 27 * C), BF16)] * 2 + [DMA((2,))],
        )(w_first, w_second)
    with jax.named_scope("rims_y"):
        ym, yp = from_owner(down, 0, -1), from_owner(up, 0, 1)
    with jax.named_scope("slabs"):
        left, right = call(slab_kernel, [slab, slab], [VMEM] * 3)(field, ym, yp)
    with jax.named_scope("rims_x"):
        xm, xp = from_owner(left, -1, 0), from_owner(right, 1, 0)
    with jax.named_scope("place"):
        base, hot_x = call(
            place_kernel,
            [((ROWS, LANES), BF16), ((256, LANES), BF16)],
            [SMEM] * 2 + [VMEM] * 4,
            [vmem((ROWS, 640), BF16)],
        )(adjacency, own, field, ym, yp, table)
    half, grads = ((128, 16, 128), F32), vmem((C, TILES_L * 128), F32)
    with jax.named_scope("middle"):
        send, padded, hidden, grad_one, col_m, col_h = call(
            main_kernel,
            [
                half, ((ROWS, LANES), BF16), ((C, OUTER), BF16), ((C, OUTER), BF16),
                ((9 * C, OUTER), BF16), ((9 * C, INNER), BF16),
            ],
            [SMEM] * 2 + [VMEM] * 7,
            [vmem((ROWS, 256), BF16), vmem((9 * C, OUTER), BF16), grads],
        )(adjacency, own, xm, xp, base, hot_x, table, one_f, two_b)
    with jax.named_scope("keep"):
        (keep,) = call(keep_kernel, [half], [SMEM] + [VMEM] * 5, [grads])(
            own, padded, grad_one, table, col_m, col_h
        )
    with jax.named_scope("pair"):
        pair = keep + swap_halves(send)
    with jax.named_scope("outputs"):
        out_feats, grad_feats, done = call(
            out_kernel,
            [((1, C, 512), BF16)] * 2 + [((8, 128), F32)],
            [ANY] + [VMEM] * 5,
            [vmem((9 * C, INNER), BF16)],
        )(pair, padded, hidden, grad_one, two_f, one_b)
    near, far = ("zl", "y", "x"), "zh"
    with jax.named_scope("sum"):
        parts = lax.all_to_all(pair, near, 0, 0, tiled=True).reshape(32, 4, 16, 128)
        (copies,) = call(
            lambda *refs: share_kernel(32, *refs), [((8, 4, 16, 128), BF16)], [VMEM] * 2
        )(parts, done)
        parts = lax.all_to_all(copies, far, 0, 0)
        (copies,) = call(
            lambda *refs: share_kernel(8, *refs), [((32, 4, 16, 128), BF16)], [VMEM]
        )(parts)
        mine = lax.all_to_all(copies, near, 0, 0).reshape(128, 16, 128)
        other = swap_halves(mine)
    grad, rows = ((C, 27 * C), F32), [vmem((C, 27 * C), F32), DMA((6,))]
    with jax.named_scope("mine"):
        begun = call(mine_kernel, [grad] * 2, [SMEM, VMEM], rows, place=ANY)(own, mine)
    with jax.named_scope("other"):
        grad_first, grad_second = call(
            other_kernel, [grad] * 2, [SMEM, VMEM, ANY, ANY], rows, place=ANY,
            input_output_aliases={2: 0, 3: 1},
        )(own, other, *begun)
    return out_feats, grad_feats, grad_first, grad_second


def solution(mesh):
    fine = Mesh(mesh.devices.reshape(8, 2, 4, 4, 2), ("zh", "zl", "y", "x", "core"))
    both = ("zh", "zl", "y", "x", "core")
    blocks = P(both, None, None)
    rows = P(both, None)
    return jax.shard_map(
        body,
        mesh=fine,
        in_specs=(blocks, blocks, rows, rows, rows, P(), P()),
        out_specs=(blocks, blocks, P(), P()),
        check_vma=False,
    )
```

```python
import jax
import jax.numpy as jnp
import numpy as np
from jax import lax
from jax.experimental import pallas as pl
from jax.experimental.pallas import tpu as pltpu
from jax.sharding import Mesh, PartitionSpec as P

C = 96
BE = 8
GRID = 8
REPS = 8
ROWS = 208
PAD = 12
LANES = 1920
OUTER = 1536
INNER = 1152
BASE = PAD * PAD + PAD
TILES_L = 21
DIRECTIONS = [(-1, -1), (0, -1), (1, -1), (-1, 0), (1, 0), (-1, 1), (0, 1), (1, 1)]
OFFSETS = [(a, b, c) for a in (-1, 0, 1) for b in (-1, 0, 1) for c in (-1, 0, 1)]
F32, BF16 = jnp.float32, jnp.bfloat16


def ints(dims, axis):
    return lax.broadcasted_iota(jnp.int32, dims, axis)


def own_voxels(first, length):
    p = ints((1, length), 1) + first
    x, y, z = p // (PAD * PAD), p // PAD % PAD, p % PAD
    inside = [jnp.logical_and(at >= 2, at < 10) for at in (x, y, z)]
    return jnp.logical_and(jnp.logical_and(inside[0], inside[1]), inside[2])


def start_inputs(feats_in, cot_in, occ_in, feats, cot, occ, sems):
    copies = [
        pltpu.make_async_copy(source, target, sems.at[number])
        for number, (source, target) in enumerate(((occ_in, occ), (feats_in, feats), (cot_in, cot)))
    ]
    for copy in copies:
        copy.start()
    return copies


def mask_inputs(copies, feats, cot, occ, field):
    copies[0].wait()
    mask = (occ[...] != 0).astype(F32).astype(BF16)
    field[2 * C :, 0:512] = jnp.broadcast_to(mask, (ROWS - 2 * C, 512))
    copies[1].wait()
    field[0:C, 0:512] = feats[0] * mask
    copies[2].wait()
    field[C : 2 * C, 0:512] = cot[0] * mask


def pack_kernel(feats_in, cot_in, occ_in, down, up, *refs):
    quarters, (field, feats, cot, occ, sems) = refs[:4], refs[4:]
    copies = start_inputs(feats_in, cot_in, occ_in, feats, cot, occ, sems)
    lane = ints((512, 256), 1)
    rim = lane % 128
    wanted = rim // 16 * 64 + rim // 8 % 2 * 8 + rim % 8 + jnp.where(lane < 128, 48, 0)
    picks = jnp.where(ints((512, 256), 0) == wanted, 1.0, 0.0).astype(BF16)
    mask_inputs(copies, feats, cot, occ, field)
    rims = jnp.dot(field[...], picks, preferred_element_type=F32).astype(BF16)
    down[...] = rims[:, 0:128]
    up[...] = rims[:, 128:256]
    for number in range(4):
        quarters[number][...] = field[:, number * 128 : (number + 1) * 128]


def slab_kernel(first, last, ym, yp, left, right):
    blank = jnp.zeros((ROWS, 64), BF16)
    left[:, 0:128] = last[...]
    left[:, 128:256] = jnp.concatenate([ym[:, 96:128], yp[:, 96:128], blank], axis=1)
    right[:, 0:128] = first[...]
    right[:, 128:256] = jnp.concatenate([ym[:, 0:32], yp[:, 0:32], blank], axis=1)


def turn_weights(copies, weights, outs):
    for copy, weight, forward, turned in zip(copies, weights, outs[0::2], outs[1::2]):
        copy.wait()
        whole = weight[...]
        across = whole.astype(F32).T.astype(BF16)
        for number in range(9):
            for dz in range(3):
                k = number * 3 + dz
                rows = slice(dz * C, (dz + 1) * C)
                columns = slice(number * C, (number + 1) * C)
                forward[rows, columns] = whole[:, k * C : (k + 1) * C]
                turned[rows, columns] = across[(26 - k) * C : (27 - k) * C, :]


def shifted_columns(source, columns, length):
    for number in range(9):
        start = (number // 3) * PAD * PAD + (number % 3) * PAD
        columns[number * C : (number + 1) * C, 0:length] = source[:, start : start + length]


def three_taps(weight, columns, length):
    parts = jnp.dot(weight[...], columns[:, 0:length], preferred_element_type=F32)
    return (
        parts[0:C]
        + pltpu.roll(parts[C : 2 * C], length - 1, 1)
        + pltpu.roll(parts[2 * C :], length - 2, 1)
    )


def weight_grad(gradient, columns, grads, tiles):
    stack = jnp.concatenate(
        [gradient, pltpu.roll(gradient, 1, 1), pltpu.roll(gradient, 2, 1)], axis=0
    ).astype(BF16)
    sums = lax.dot_general(
        stack, columns, (((1,), (1,)), ((), ())), preferred_element_type=F32
    ) * (1.0 / 512.0)
    for number in range(9):
        for dz in range(3):
            k = number * 3 + dz
            grads[:, k * C : (k + 1) * C] = sums[
                dz * C : (dz + 1) * C, number * C : (number + 1) * C
            ]
    grads[:, 27 * C :] = jnp.zeros((C, TILES_L * 128 - 27 * C), F32)
    for tile in range(6 * TILES_L):
        row, lane = tile // TILES_L * 16, tile % TILES_L * 128
        tiles[tile] = grads[row : row + 16, lane : lane + 128]
    tiles[6 * TILES_L :] = jnp.zeros((128 - 6 * TILES_L, 16, 128), F32)


def relative_owners(adj, own):
    owners = [adj[0, k] for k in range(27)]
    return [jnp.where(block < 0, 99, block // REPS - own[0]) for block in owners]


def among(relative, steps):
    found = relative[0] == steps[0]
    for value in relative:
        for step in steps:
            found = jnp.logical_or(found, value == step)
    return found


def prepare_kernel(
    adj, own, first_in, second_in,
    first_forward, first_turned, second_forward, second_turned, places, low, side,
    first, second, weight_sems,
):
    weight_copies = [
        pltpu.make_async_copy(first_in, first, weight_sems.at[0]),
        pltpu.make_async_copy(second_in, second, weight_sems.at[1]),
    ]
    for copy in weight_copies:
        copy.start()
    relative = relative_owners(adj, own)
    from_left = among(relative, [-1 - GRID, -1, -1 + GRID])
    side[...] = jnp.full(side.shape, jnp.where(from_left, 1.0, 0.0), F32).astype(BF16)
    from_low = among(relative, [-GRID])
    low[...] = jnp.full(low.shape, jnp.where(from_low, 1.0, 0.0), F32).astype(BF16)
    p = ints((1, LANES), 1)
    at = [p // (PAD * PAD) - 2, p // PAD % PAD - 2, p % PAD - 2]
    out = [jnp.where(v < 0, 0, jnp.where(v >= BE, 2, 1)) for v in at]
    site = jnp.where(p < PAD**3, out[0] * 9 + out[1] * 3 + out[2], 27)
    x, y, z = (jnp.where(v < 0, v + BE, jnp.where(v >= BE, v - BE, v)) for v in at)
    which = jnp.full((1, LANES), 99, jnp.int32)
    for k in range(27):
        which = jnp.where(site == k, relative[k], which)
    place = jnp.where(which == 0, x * 64 + y * 8 + z, -1)
    for sx, sy in DIRECTIONS:
        nx, ny = (x - 6 if sx < 0 else x), (y - 6 if sy < 0 else y)
        if sx == 0:
            there = 512 + x * 16 + ny * 8 + z
        elif sy == 0:
            there = 640 + nx * 64 + y * 8 + z
        else:
            there = (768 if sy < 0 else 800) + nx * 16 + ny * 8 + z
        place = jnp.where(which == sx + GRID * sy, there, place)
    places[...] = jnp.broadcast_to(place, places.shape)
    turn_weights(
        weight_copies, (first, second), (first_forward, first_turned, second_forward, second_turned)
    )


def either(flag, one, other):
    return one * flag + other * (1.0 - flag.astype(F32)).astype(BF16)


def place_kernel(q0, q1, q2, q3, ym, yp, places, low, base, hot_x, sources):
    for number, quarter in enumerate((q0, q1, q2, q3)):
        sources[:, number * 128 : (number + 1) * 128] = quarter[...]
    sources[:, 512:640] = either(low[0:1, :], ym[...], yp[...])
    width = 384
    for part in range(LANES // width):
        cut = slice(part * width, (part + 1) * width)
        hot = jnp.where(ints((896, width), 0) == places[0:1, cut], 1.0, 0.0).astype(BF16)
        hot_x[:, cut] = hot[640:896]
        base[:, cut] = jnp.dot(
            sources[...], hot[0:640], preferred_element_type=F32
        ).astype(BF16)


def main_kernel(
    own, xm, xp, base, hot_x, side, w_one, w_two,
    send, padded, hidden, grad_one, inner, columns,
    col_g, grads,
):
    slab = either(side[0:1, :], xm[...], xp[...])
    width = 384
    for part in range(LANES // width):
        cut = slice(part * width, (part + 1) * width)
        near = jnp.dot(slab, hot_x[:, cut], preferred_element_type=F32)
        padded[:, cut] = (base[:, cut].astype(F32) + near).astype(BF16)
    shifted_columns(padded[0:C, :], columns.at[0], OUTER)
    shifted_columns(padded[C : 2 * C, :], col_g, OUTER)
    mask = padded[2 * C : 2 * C + 1, BASE + 1 : BASE + 1 + OUTER].astype(F32)
    pre = three_taps(w_one, columns.at[0], OUTER)
    sig = jax.nn.sigmoid(pre)
    hidden[...] = (pre * sig * mask).astype(BF16)
    back = three_taps(w_two, col_g, OUTER)
    grad = (back * mask * sig * (1.0 + pre * (1.0 - sig))).astype(BF16)
    grad_one[...] = grad
    shifted_columns(hidden[...], columns.at[1], INNER)
    columns[1, :, INNER:OUTER] = jnp.zeros((9 * C, OUTER - INNER), BF16)
    kept = jnp.where(own_voxels(BASE + 1, OUTER), 1.0, 0.0)
    inner[0] = (grad.astype(F32) * kept).astype(BF16)
    start = 2 * (BASE + 1)
    kept = jnp.where(own_voxels(start, INNER), 1.0, 0.0)
    grad_two = padded[C : 2 * C, start : start + INNER].astype(F32)
    inner[1, :, 0:INNER] = (grad_two * kept).astype(BF16)
    inner[1, :, INNER:OUTER] = jnp.zeros((C, OUTER - INNER), BF16)
    weight_grad(inner[1 - own[1]].astype(F32), columns[1 - own[1]], grads, send)


def keep_kernel(own, inner, columns, keep, grads):
    weight_grad(inner[own[1]].astype(F32), columns[own[1]], grads, keep)


def out_kernel(after, padded, hidden, grad_one, w_two, w_one, out_feats, grad_feats, done, columns):
    done[...] = jnp.zeros((8, 128), F32)
    voxel = ints((INNER, 512), 1)
    inner = voxel // 64 * (PAD * PAD) + voxel // 8 % 8 * PAD + voxel % 8
    squeeze = jnp.where(ints((INNER, 512), 0) == inner, 1.0, 0.0).astype(BF16)
    start = 2 * (BASE + 1)
    mask = padded[2 * C : 2 * C + 1, start : start + INNER].astype(F32)
    for first, field, weight, out in (
        (0, hidden, w_two, out_feats),
        (C, grad_one, w_one, grad_feats),
    ):
        shifted_columns(field[...], columns, INNER)
        pre = three_taps(weight, columns, INNER)
        kept = padded[first : first + C, start : start + INNER].astype(F32)
        wide = (kept + pre * mask).astype(BF16)
        out[0] = jnp.dot(wide, squeeze, preferred_element_type=F32).astype(BF16)


def share_kernel(count, parts, *refs):
    total = parts[0].astype(F32)
    for number in range(1, count):
        total = total + parts[number].astype(F32)
    copies = refs[-1]
    for number in range(copies.shape[0]):
        copies[number] = total.astype(BF16)


def write_half(half, out, rows, sems):
    copies = []
    for row in range(6):
        for lane in range(TILES_L):
            last = min((lane + 1) * 128, 27 * C)
            part = half[row * TILES_L + lane].astype(F32)
            rows[row * 16 : row * 16 + 16, lane * 128 : last] = part[:, : last - lane * 128]
        at = pl.ds(row * 16, 16)
        copies.append(pltpu.make_async_copy(rows.at[at], out.at[at], sems.at[row]))
        copies[-1].start()
    for copy in copies:
        copy.wait()


def mine_kernel(own, half, first, second, rows, sems):
    @pl.when(own[1] == 0)
    def _():
        write_half(half, first, rows, sems)

    @pl.when(own[1] != 0)
    def _():
        write_half(half, second, rows, sems)


def other_kernel(own, half, first_in, second_in, first, second, rows, sems):
    @pl.when(own[1] == 0)
    def _():
        write_half(half, second, rows, sems)

    @pl.when(own[1] != 0)
    def _():
        write_half(half, first, rows, sems)


VMEM = pl.BlockSpec(memory_space=pltpu.VMEM)
SMEM = pl.BlockSpec(memory_space=pltpu.SMEM)
HBM = pl.BlockSpec(memory_space=pltpu.HBM)
ANY = pl.BlockSpec(memory_space=pl.ANY)
DMA = pltpu.SemaphoreType.DMA
MIB = 1024 * 1024
PACK, PREPARE = int(53.58 * MIB), int(51.4 * MIB)


def call(kernel, outs, specs, scratch=(), place=VMEM, limit=40 * MIB, **options):
    return pl.pallas_call(
        kernel,
        out_shape=[jax.ShapeDtypeStruct(*out) for out in outs],
        in_specs=specs,
        out_specs=[place] * len(outs),
        scratch_shapes=scratch,
        compiler_params=pltpu.CompilerParams(vmem_limit_bytes=limit),
        **options,
    )


def from_owner(value, sx, sy):
    pairs = []
    for owner in range(GRID * GRID):
        column, row = owner % GRID + sx, owner // GRID + sy
        if 0 <= column < GRID and 0 <= row < GRID:
            pairs.append((row * GRID + column, owner))
    return lax.ppermute(value, ("zh", "zl", "y"), pairs)


def swap_halves(value):
    return lax.ppermute(value, "core", [(0, 1), (1, 0)])


def body(feats, cotangent, occupancy, counts, adjacency, w_first, w_second):
    own = jnp.stack([lax.axis_index(("zh", "zl", "y")), lax.axis_index("core")]).astype(jnp.int32)
    rim, slab, turned = ((ROWS, 128), BF16), ((ROWS, 256), BF16), ((3 * C, 9 * C), BF16)
    vmem = pltpu.VMEM
    inputs = [
        vmem((1, C, 512), BF16), vmem((1, C, 512), BF16), vmem((1, 512), jnp.int32), DMA((3,))
    ]
    with jax.named_scope("pack"):
        down, up, *quarters = call(
            pack_kernel, [rim] * 6, [HBM] * 3, [vmem((ROWS, 512), BF16)] + inputs, limit=PACK
        )(feats, cotangent, occupancy)
    with jax.named_scope("prepare"):
        one_f, one_b, two_f, two_b, places, low, side = call(
            prepare_kernel,
            [turned] * 4
            + [((8, LANES), jnp.int32), ((16, 128), BF16), ((16, 256), BF16)],
            [SMEM] * 2 + [HBM] * 2,
            [vmem((C, 27 * C), BF16)] * 2 + [DMA((2,))],
            limit=PREPARE,
        )(adjacency, own, w_first, w_second)
    with jax.named_scope("rims_y"):
        ym, yp = from_owner(down, 0, -1), from_owner(up, 0, 1)
    with jax.named_scope("slabs"):
        left, right = call(slab_kernel, [slab, slab], [VMEM] * 4)(quarters[0], quarters[3], ym, yp)
    with jax.named_scope("rims_x"):
        xm, xp = from_owner(left, -1, 0), from_owner(right, 1, 0)
    with jax.named_scope("place"):
        base, hot_x = call(
            place_kernel,
            [((ROWS, LANES), BF16), ((256, LANES), BF16)],
            [VMEM] * 8,
            [vmem((ROWS, 640), BF16)],
        )(*quarters, ym, yp, places, low)
    half, grads = ((128, 16, 128), F32), vmem((C, TILES_L * 128), F32)
    outer = ((C, OUTER), BF16)
    with jax.named_scope("middle"):
        send, padded, hidden, grad_one, inner, columns = call(
            main_kernel,
            [
                half, ((ROWS, LANES), BF16), outer, outer,
                ((2, C, OUTER), BF16), ((2, 9 * C, OUTER), BF16),
            ],
            [SMEM] + [VMEM] * 7,
            [vmem((9 * C, OUTER), BF16), grads],
        )(own, xm, xp, base, hot_x, side, one_f, two_b)
    with jax.named_scope("keep"):
        (keep,) = call(keep_kernel, [half], [SMEM] + [VMEM] * 2, [grads])(own, inner, columns)
    with jax.named_scope("pair"):
        pair = keep + swap_halves(send)
    near, far = ("zl", "y", "x"), "zh"
    with jax.named_scope("sum"):
        parts = lax.all_to_all(pair, near, 0, 0, tiled=True).reshape(32, 4, 16, 128)
        (copies,) = call(
            lambda *refs: share_kernel(32, *refs), [((8, 4, 16, 128), BF16)], [VMEM]
        )(parts)
        parts = lax.all_to_all(copies, far, 0, 0)
    with jax.named_scope("outputs"):
        out_feats, grad_feats, done = call(
            out_kernel,
            [((1, C, 512), BF16)] * 2 + [((8, 128), F32)],
            [ANY] + [VMEM] * 5,
            [vmem((9 * C, INNER), BF16)],
        )(copies, padded, hidden, grad_one, two_f, one_b)
    with jax.named_scope("shares"):
        (copies,) = call(
            lambda *refs: share_kernel(8, *refs), [((32, 4, 16, 128), BF16)], [VMEM] * 2
        )(parts, done)
        mine = lax.all_to_all(copies, near, 0, 0).reshape(128, 16, 128)
        other = swap_halves(mine)
    grad, rows = ((C, 27 * C), F32), [vmem((C, 27 * C), F32), DMA((6,))]
    with jax.named_scope("mine"):
        begun = call(mine_kernel, [grad] * 2, [SMEM, VMEM], rows, place=ANY)(own, mine)
    with jax.named_scope("other"):
        grad_first, grad_second = call(
            other_kernel, [grad] * 2, [SMEM, VMEM, ANY, ANY], rows, place=ANY,
            input_output_aliases={2: 0, 3: 1},
        )(own, other, *begun)
    return out_feats, grad_feats, grad_first, grad_second


def solution(mesh):
    fine = Mesh(mesh.devices.reshape(8, 2, 4, 4, 2), ("zh", "zl", "y", "x", "core"))
    both = ("zh", "zl", "y", "x", "core")
    blocks = P(both, None, None)
    rows = P(both, None)
    return jax.shard_map(
        body,
        mesh=fine,
        in_specs=(blocks, blocks, rows, rows, rows, P(), P()),
        out_specs=(blocks, blocks, P(), P()),
        check_vma=False,
    )
```

```python
import jax
import jax.numpy as jnp
import numpy as np
from jax import lax
from jax.experimental import pallas as pl
from jax.experimental.pallas import tpu as pltpu
from jax.sharding import Mesh, PartitionSpec as P

C = 96
BE = 8
GRID = 8
REPS = 8
ROWS = 208
PAD = 12
LANES = 1920
OUTER = 1536
INNER = 1152
BASE = PAD * PAD + PAD
TILES_L = 21
DIRECTIONS = [(-1, -1), (0, -1), (1, -1), (-1, 0), (1, 0), (-1, 1), (0, 1), (1, 1)]
OFFSETS = [(a, b, c) for a in (-1, 0, 1) for b in (-1, 0, 1) for c in (-1, 0, 1)]
F32, BF16 = jnp.float32, jnp.bfloat16


def ints(dims, axis):
    return lax.broadcasted_iota(jnp.int32, dims, axis)


def own_voxels(first, length):
    p = ints((1, length), 1) + first
    x, y, z = p // (PAD * PAD), p // PAD % PAD, p % PAD
    inside = [jnp.logical_and(at >= 2, at < 10) for at in (x, y, z)]
    return jnp.logical_and(jnp.logical_and(inside[0], inside[1]), inside[2])


def start_inputs(feats_in, cot_in, occ_in, feats, cot, occ, sems):
    copies = [
        pltpu.make_async_copy(source, target, sems.at[number])
        for number, (source, target) in enumerate(((occ_in, occ), (feats_in, feats), (cot_in, cot)))
    ]
    for copy in copies:
        copy.start()
    return copies


def mask_inputs(copies, feats, cot, occ, field):
    copies[0].wait()
    mask = (occ[...] != 0).astype(F32).astype(BF16)
    field[2 * C :, 0:512] = jnp.broadcast_to(mask, (ROWS - 2 * C, 512))
    copies[1].wait()
    field[0:C, 0:512] = feats[0] * mask
    copies[2].wait()
    field[C : 2 * C, 0:512] = cot[0] * mask


def pack_kernel(feats_in, cot_in, occ_in, down, up, *refs):
    quarters, (field, feats, cot, occ, sems) = refs[:4], refs[4:]
    copies = start_inputs(feats_in, cot_in, occ_in, feats, cot, occ, sems)
    lane = ints((512, 256), 1)
    rim = lane % 128
    wanted = rim // 16 * 64 + rim // 8 % 2 * 8 + rim % 8 + jnp.where(lane < 128, 48, 0)
    picks = jnp.where(ints((512, 256), 0) == wanted, 1.0, 0.0).astype(BF16)
    mask_inputs(copies, feats, cot, occ, field)
    rims = jnp.dot(field[...], picks, preferred_element_type=F32).astype(BF16)
    down[...] = rims[:, 0:128]
    up[...] = rims[:, 128:256]
    for number in range(4):
        quarters[number][...] = field[:, number * 128 : (number + 1) * 128]


def slab_kernel(after, first, last, ym, yp, left, right):
    blank = jnp.zeros((ROWS, 64), BF16)
    left[:, 0:128] = last[...]
    left[:, 128:256] = jnp.concatenate([ym[:, 96:128], yp[:, 96:128], blank], axis=1)
    right[:, 0:128] = first[...]
    right[:, 128:256] = jnp.concatenate([ym[:, 0:32], yp[:, 0:32], blank], axis=1)


def tap_blocks():
    for number in range(9):
        for dz in range(3):
            k = number * 3 + dz
            yield k, slice(dz * C, (dz + 1) * C), slice(number * C, (number + 1) * C)


def forward_weight(weight, out):
    whole = weight[...]
    for k, rows, columns in tap_blocks():
        out[rows, columns] = whole[:, k * C : (k + 1) * C]


def turned_weight(weight, out):
    across = weight[...].astype(F32).T.astype(BF16)
    for k, rows, columns in tap_blocks():
        out[rows, columns] = across[(26 - k) * C : (27 - k) * C, :]


def start_weights(first_in, second_in, first, second, sems):
    copies = [
        pltpu.make_async_copy(first_in, first, sems.at[0]),
        pltpu.make_async_copy(second_in, second, sems.at[1]),
    ]
    for copy in copies:
        copy.start()
    return copies


def late_weight_kernel(after, first_in, second_in, second_forward, first_turned, first, second, sems):
    copies = start_weights(first_in, second_in, first, second, sems)
    copies[1].wait()
    forward_weight(second, second_forward)
    copies[0].wait()
    turned_weight(first, first_turned)


def shifted_columns(source, columns, length):
    for number in range(9):
        start = (number // 3) * PAD * PAD + (number % 3) * PAD
        columns[number * C : (number + 1) * C, 0:length] = source[:, start : start + length]


def three_taps(weight, columns, length):
    parts = jnp.dot(weight[...], columns[:, 0:length], preferred_element_type=F32)
    return (
        parts[0:C]
        + pltpu.roll(parts[C : 2 * C], length - 1, 1)
        + pltpu.roll(parts[2 * C :], length - 2, 1)
    )


def weight_grad(gradient, columns, grads, tiles):
    stack = jnp.concatenate(
        [gradient, pltpu.roll(gradient, 1, 1), pltpu.roll(gradient, 2, 1)], axis=0
    ).astype(BF16)
    sums = lax.dot_general(
        stack, columns, (((1,), (1,)), ((), ())), preferred_element_type=F32
    ) * (1.0 / 512.0)
    for number in range(9):
        for dz in range(3):
            k = number * 3 + dz
            grads[:, k * C : (k + 1) * C] = sums[
                dz * C : (dz + 1) * C, number * C : (number + 1) * C
            ]
    grads[:, 27 * C :] = jnp.zeros((C, TILES_L * 128 - 27 * C), F32)
    for tile in range(6 * TILES_L):
        row, lane = tile // TILES_L * 16, tile % TILES_L * 128
        tiles[tile] = grads[row : row + 16, lane : lane + 128]
    tiles[6 * TILES_L :] = jnp.zeros((128 - 6 * TILES_L, 16, 128), F32)


def relative_owners(adj, own):
    owners = [adj[0, k] for k in range(27)]
    return [jnp.where(block < 0, 99, block // REPS - own[0]) for block in owners]


def among(relative, steps):
    found = relative[0] == steps[0]
    for value in relative:
        for step in steps:
            found = jnp.logical_or(found, value == step)
    return found


def prepare_kernel(
    adj, own, first_in, second_in, first_forward, second_turned, places, low, side,
    first, second, sems,
):
    copies = start_weights(first_in, second_in, first, second, sems)
    relative = relative_owners(adj, own)
    from_left = among(relative, [-1 - GRID, -1, -1 + GRID])
    side[...] = jnp.full(side.shape, jnp.where(from_left, 1.0, 0.0), F32).astype(BF16)
    from_low = among(relative, [-GRID])
    low[...] = jnp.full(low.shape, jnp.where(from_low, 1.0, 0.0), F32).astype(BF16)
    p = ints((1, LANES), 1)
    at = [p // (PAD * PAD) - 2, p // PAD % PAD - 2, p % PAD - 2]
    out = [jnp.where(v < 0, 0, jnp.where(v >= BE, 2, 1)) for v in at]
    site = jnp.where(p < PAD**3, out[0] * 9 + out[1] * 3 + out[2], 27)
    x, y, z = (jnp.where(v < 0, v + BE, jnp.where(v >= BE, v - BE, v)) for v in at)
    which = jnp.full((1, LANES), 99, jnp.int32)
    for k in range(27):
        which = jnp.where(site == k, relative[k], which)
    place = jnp.where(which == 0, x * 64 + y * 8 + z, -1)
    for sx, sy in DIRECTIONS:
        nx, ny = (x - 6 if sx < 0 else x), (y - 6 if sy < 0 else y)
        if sx == 0:
            there = 512 + x * 16 + ny * 8 + z
        elif sy == 0:
            there = 640 + nx * 64 + y * 8 + z
        else:
            there = (768 if sy < 0 else 800) + nx * 16 + ny * 8 + z
        place = jnp.where(which == sx + GRID * sy, there, place)
    places[...] = jnp.broadcast_to(place, places.shape)
    copies[0].wait()
    forward_weight(first, first_forward)
    copies[1].wait()
    turned_weight(second, second_turned)


def either(flag, one, other):
    return one * flag + other * (1.0 - flag.astype(F32)).astype(BF16)


def place_kernel(q0, q1, q2, q3, ym, yp, places, low, base, hot_x, sources):
    for number, quarter in enumerate((q0, q1, q2, q3)):
        sources[:, number * 128 : (number + 1) * 128] = quarter[...]
    sources[:, 512:640] = either(low[0:1, :], ym[...], yp[...])
    width = 384
    for part in range(LANES // width):
        cut = slice(part * width, (part + 1) * width)
        hot = jnp.where(ints((896, width), 0) == places[0:1, cut], 1.0, 0.0).astype(BF16)
        hot_x[:, cut] = hot[640:896]
        base[:, cut] = jnp.dot(
            sources[...], hot[0:640], preferred_element_type=F32
        ).astype(BF16)


def main_kernel(
    own, xm, xp, base, hot_x, side, w_one, w_two,
    send, padded, hidden, grad_one, inner, columns,
    col_g, grads,
):
    slab = either(side[0:1, :], xm[...], xp[...])
    width = 384
    for part in range(LANES // width):
        cut = slice(part * width, (part + 1) * width)
        near = jnp.dot(slab, hot_x[:, cut], preferred_element_type=F32)
        padded[:, cut] = (base[:, cut].astype(F32) + near).astype(BF16)
    shifted_columns(padded[0:C, :], columns.at[0], OUTER)
    shifted_columns(padded[C : 2 * C, :], col_g, OUTER)
    mask = padded[2 * C : 2 * C + 1, BASE + 1 : BASE + 1 + OUTER].astype(F32)
    pre = three_taps(w_one, columns.at[0], OUTER)
    sig = jax.nn.sigmoid(pre)
    hidden[...] = (pre * sig * mask).astype(BF16)
    back = three_taps(w_two, col_g, OUTER)
    grad = (back * mask * sig * (1.0 + pre * (1.0 - sig))).astype(BF16)
    grad_one[...] = grad
    shifted_columns(hidden[...], columns.at[1], INNER)
    columns[1, :, INNER:OUTER] = jnp.zeros((9 * C, OUTER - INNER), BF16)
    kept = jnp.where(own_voxels(BASE + 1, OUTER), 1.0, 0.0)
    inner[0] = (grad.astype(F32) * kept).astype(BF16)
    start = 2 * (BASE + 1)
    kept = jnp.where(own_voxels(start, INNER), 1.0, 0.0)
    grad_two = padded[C : 2 * C, start : start + INNER].astype(F32)
    inner[1, :, 0:INNER] = (grad_two * kept).astype(BF16)
    inner[1, :, INNER:OUTER] = jnp.zeros((C, OUTER - INNER), BF16)
    weight_grad(inner[1 - own[1]].astype(F32), columns[1 - own[1]], grads, send)


def keep_kernel(own, inner, columns, keep, grads):
    weight_grad(inner[own[1]].astype(F32), columns[own[1]], grads, keep)


def out_kernel(after, padded, hidden, grad_one, w_two, w_one, out_feats, grad_feats, done, columns):
    done[...] = jnp.zeros((8, 128), F32)
    voxel = ints((INNER, 512), 1)
    inner = voxel // 64 * (PAD * PAD) + voxel // 8 % 8 * PAD + voxel % 8
    squeeze = jnp.where(ints((INNER, 512), 0) == inner, 1.0, 0.0).astype(BF16)
    start = 2 * (BASE + 1)
    mask = padded[2 * C : 2 * C + 1, start : start + INNER].astype(F32)
    for first, field, weight, out in (
        (0, hidden, w_two, out_feats),
        (C, grad_one, w_one, grad_feats),
    ):
        shifted_columns(field[...], columns, INNER)
        pre = three_taps(weight, columns, INNER)
        kept = padded[first : first + C, start : start + INNER].astype(F32)
        wide = (kept + pre * mask).astype(BF16)
        out[0] = jnp.dot(wide, squeeze, preferred_element_type=F32).astype(BF16)


def share_kernel(count, parts, *refs):
    total = parts[0].astype(F32)
    for number in range(1, count):
        total = total + parts[number].astype(F32)
    copies = refs[-1]
    for number in range(copies.shape[0]):
        copies[number] = total.astype(BF16)


def write_half(half, out, rows, sems):
    copies = []
    for row in range(6):
        for lane in range(TILES_L):
            last = min((lane + 1) * 128, 27 * C)
            part = half[row * TILES_L + lane].astype(F32)
            rows[row * 16 : row * 16 + 16, lane * 128 : last] = part[:, : last - lane * 128]
        at = pl.ds(row * 16, 16)
        copies.append(pltpu.make_async_copy(rows.at[at], out.at[at], sems.at[row]))
        copies[-1].start()
    for copy in copies:
        copy.wait()


def mine_kernel(own, half, first, second, rows, sems):
    @pl.when(own[1] == 0)
    def _():
        write_half(half, first, rows, sems)

    @pl.when(own[1] != 0)
    def _():
        write_half(half, second, rows, sems)


def other_kernel(own, half, first_in, second_in, first, second, rows, sems):
    @pl.when(own[1] == 0)
    def _():
        write_half(half, second, rows, sems)

    @pl.when(own[1] != 0)
    def _():
        write_half(half, first, rows, sems)


VMEM = pl.BlockSpec(memory_space=pltpu.VMEM)
SMEM = pl.BlockSpec(memory_space=pltpu.SMEM)
HBM = pl.BlockSpec(memory_space=pltpu.HBM)
ANY = pl.BlockSpec(memory_space=pl.ANY)
DMA = pltpu.SemaphoreType.DMA
MIB = 1024 * 1024
PACK, PREPARE, LATE = int(53.58 * MIB), int(52.4 * MIB), int(52.5 * MIB)


def call(kernel, outs, specs, scratch=(), place=VMEM, limit=40 * MIB, **options):
    return pl.pallas_call(
        kernel,
        out_shape=[jax.ShapeDtypeStruct(*out) for out in outs],
        in_specs=specs,
        out_specs=[place] * len(outs),
        scratch_shapes=scratch,
        compiler_params=pltpu.CompilerParams(vmem_limit_bytes=limit),
        **options,
    )


def from_owner(value, sx, sy):
    pairs = []
    for owner in range(GRID * GRID):
        column, row = owner % GRID + sx, owner // GRID + sy
        if 0 <= column < GRID and 0 <= row < GRID:
            pairs.append((row * GRID + column, owner))
    return lax.ppermute(value, ("zh", "zl", "y"), pairs)


def swap_halves(value):
    return lax.ppermute(value, "core", [(0, 1), (1, 0)])


def body(feats, cotangent, occupancy, counts, adjacency, w_first, w_second):
    own = jnp.stack([lax.axis_index(("zh", "zl", "y")), lax.axis_index("core")]).astype(jnp.int32)
    rim, slab, turned = ((ROWS, 128), BF16), ((ROWS, 256), BF16), ((3 * C, 9 * C), BF16)
    vmem = pltpu.VMEM
    inputs = [
        vmem((1, C, 512), BF16), vmem((1, C, 512), BF16), vmem((1, 512), jnp.int32), DMA((3,))
    ]
    weights = [vmem((C, 27 * C), BF16)] * 2 + [DMA((2,))]
    with jax.named_scope("pack"):
        down, up, *quarters = call(
            pack_kernel, [rim] * 6, [HBM] * 3, [vmem((ROWS, 512), BF16)] + inputs, limit=PACK
        )(feats, cotangent, occupancy)
    with jax.named_scope("prepare"):
        one_f, two_b, places, low, side = call(
            prepare_kernel,
            [turned] * 2
            + [((8, LANES), jnp.int32), ((16, 128), BF16), ((16, 256), BF16)],
            [SMEM] * 2 + [HBM] * 2,
            weights,
            limit=PREPARE,
        )(adjacency, own, w_first, w_second)
    with jax.named_scope("rims_y"):
        ym, yp = from_owner(down, 0, -1), from_owner(up, 0, 1)
    with jax.named_scope("slabs"):
        left, right = call(slab_kernel, [slab, slab], [VMEM] * 5)(
            side, quarters[0], quarters[3], ym, yp
        )
    with jax.named_scope("rims_x"):
        xm, xp = from_owner(left, -1, 0), from_owner(right, 1, 0)
    with jax.named_scope("place"):
        base, hot_x = call(
            place_kernel,
            [((ROWS, LANES), BF16), ((256, LANES), BF16)],
            [VMEM] * 8,
            [vmem((ROWS, 640), BF16)],
        )(*quarters, ym, yp, places, low)
    half, grads = ((128, 16, 128), F32), vmem((C, TILES_L * 128), F32)
    outer = ((C, OUTER), BF16)
    with jax.named_scope("middle"):
        send, padded, hidden, grad_one, inner, columns = call(
            main_kernel,
            [
                half, ((ROWS, LANES), BF16), outer, outer,
                ((2, C, OUTER), BF16), ((2, 9 * C, OUTER), BF16),
            ],
            [SMEM] + [VMEM] * 7,
            [vmem((9 * C, OUTER), BF16), grads],
        )(own, xm, xp, base, hot_x, side, one_f, two_b)
    with jax.named_scope("keep"):
        (keep,) = call(keep_kernel, [half], [SMEM] + [VMEM] * 2, [grads])(own, inner, columns)
    with jax.named_scope("pair"):
        pair = keep + swap_halves(send)
    near, far = ("zl", "y", "x"), "zh"
    with jax.named_scope("sum"):
        parts = lax.all_to_all(pair, near, 0, 0, tiled=True).reshape(32, 4, 16, 128)
        (copies,) = call(
            lambda *refs: share_kernel(32, *refs), [((8, 4, 16, 128), BF16)], [VMEM]
        )(parts)
        parts = lax.all_to_all(copies, far, 0, 0)
    with jax.named_scope("late_weights"):
        two_f, one_b = call(
            late_weight_kernel, [turned] * 2, [ANY] + [HBM] * 2, weights, limit=LATE
        )(copies, w_first, w_second)
    with jax.named_scope("outputs"):
        out_feats, grad_feats, done = call(
            out_kernel,
            [((1, C, 512), BF16)] * 2 + [((8, 128), F32)],
            [ANY] + [VMEM] * 5,
            [vmem((9 * C, INNER), BF16)],
        )(copies, padded, hidden, grad_one, two_f, one_b)
    with jax.named_scope("shares"):
        (copies,) = call(
            lambda *refs: share_kernel(8, *refs), [((32, 4, 16, 128), BF16)], [VMEM] * 2
        )(parts, done)
        mine = lax.all_to_all(copies, near, 0, 0).reshape(128, 16, 128)
        other = swap_halves(mine)
    grad, rows = ((C, 27 * C), F32), [vmem((C, 27 * C), F32), DMA((6,))]
    with jax.named_scope("mine"):
        begun = call(mine_kernel, [grad] * 2, [SMEM, VMEM], rows, place=ANY)(own, mine)
    with jax.named_scope("other"):
        grad_first, grad_second = call(
            other_kernel, [grad] * 2, [SMEM, VMEM, ANY, ANY], rows, place=ANY,
            input_output_aliases={2: 0, 3: 1},
        )(own, other, *begun)
    return out_feats, grad_feats, grad_first, grad_second


def solution(mesh):
    fine = Mesh(mesh.devices.reshape(8, 2, 4, 4, 2), ("zh", "zl", "y", "x", "core"))
    both = ("zh", "zl", "y", "x", "core")
    blocks = P(both, None, None)
    rows = P(both, None)
    return jax.shard_map(
        body,
        mesh=fine,
        in_specs=(blocks, blocks, rows, rows, rows, P(), P()),
        out_specs=(blocks, blocks, P(), P()),
        check_vma=False,
    )
```

```python
import jax
import jax.numpy as jnp
import numpy as np
from jax import lax
from jax.experimental import pallas as pl
from jax.experimental.pallas import tpu as pltpu
from jax.sharding import Mesh, PartitionSpec as P

C = 96
BE = 8
GRID = 8
REPS = 8
ROWS = 208
PAD = 12
LANES = 1920
OUTER = 1536
INNER = 1152
BASE = PAD * PAD + PAD
TILES_L = 21
DIRECTIONS = [(-1, -1), (0, -1), (1, -1), (-1, 0), (1, 0), (-1, 1), (0, 1), (1, 1)]
OFFSETS = [(a, b, c) for a in (-1, 0, 1) for b in (-1, 0, 1) for c in (-1, 0, 1)]
F32, BF16 = jnp.float32, jnp.bfloat16


def ints(dims, axis):
    return lax.broadcasted_iota(jnp.int32, dims, axis)


def own_voxels(first, length):
    p = ints((1, length), 1) + first
    x, y, z = p // (PAD * PAD), p // PAD % PAD, p % PAD
    inside = [jnp.logical_and(at >= 2, at < 10) for at in (x, y, z)]
    return jnp.logical_and(jnp.logical_and(inside[0], inside[1]), inside[2])


def start_inputs(feats_in, cot_in, occ_in, feats, cot, occ, sems):
    copies = [
        pltpu.make_async_copy(source, target, sems.at[number])
        for number, (source, target) in enumerate(((occ_in, occ), (feats_in, feats), (cot_in, cot)))
    ]
    for copy in copies:
        copy.start()
    return copies


def mask_inputs(copies, feats, cot, occ, field):
    copies[0].wait()
    mask = (occ[...] != 0).astype(F32).astype(BF16)
    field[2 * C :, 0:512] = jnp.broadcast_to(mask, (ROWS - 2 * C, 512))
    copies[1].wait()
    field[0:C, 0:512] = feats[0] * mask
    copies[2].wait()
    field[C : 2 * C, 0:512] = cot[0] * mask


def pack_kernel(feats_in, cot_in, occ_in, down, up, *refs):
    quarters, (field, feats, cot, occ, sems) = refs[:4], refs[4:]
    copies = start_inputs(feats_in, cot_in, occ_in, feats, cot, occ, sems)
    lane = ints((512, 256), 1)
    rim = lane % 128
    wanted = rim // 16 * 64 + rim // 8 % 2 * 8 + rim % 8 + jnp.where(lane < 128, 48, 0)
    picks = jnp.where(ints((512, 256), 0) == wanted, 1.0, 0.0).astype(BF16)
    mask_inputs(copies, feats, cot, occ, field)
    rims = jnp.dot(field[...], picks, preferred_element_type=F32).astype(BF16)
    down[...] = rims[:, 0:128]
    up[...] = rims[:, 128:256]
    for number in range(4):
        quarters[number][...] = field[:, number * 128 : (number + 1) * 128]


def slab_kernel(after, first, last, ym, yp, left, right):
    blank = jnp.zeros((ROWS, 64), BF16)
    left[:, 0:128] = last[...]
    left[:, 128:256] = jnp.concatenate([ym[:, 96:128], yp[:, 96:128], blank], axis=1)
    right[:, 0:128] = first[...]
    right[:, 128:256] = jnp.concatenate([ym[:, 0:32], yp[:, 0:32], blank], axis=1)


def tap_blocks():
    for number in range(9):
        for dz in range(3):
            k = number * 3 + dz
            yield k, slice(dz * C, (dz + 1) * C), slice(number * C, (number + 1) * C)


def forward_weight(weight, out):
    whole = weight[...]
    for k, rows, columns in tap_blocks():
        out[rows, columns] = whole[:, k * C : (k + 1) * C]


def turned_weight(weight, out):
    across = weight[...].astype(F32).T.astype(BF16)
    for k, rows, columns in tap_blocks():
        out[rows, columns] = across[(26 - k) * C : (27 - k) * C, :]


def start_weights(first_in, second_in, first, second, sems):
    copies = [
        pltpu.make_async_copy(first_in, first, sems.at[0]),
        pltpu.make_async_copy(second_in, second, sems.at[1]),
    ]
    for copy in copies:
        copy.start()
    return copies


def late_weight_kernel(after, first_in, second_in, second_forward, first_turned, first, second, sems):
    copies = start_weights(first_in, second_in, first, second, sems)
    copies[1].wait()
    forward_weight(second, second_forward)
    copies[0].wait()
    turned_weight(first, first_turned)


def shifted_columns(source, columns, length):
    for number in range(9):
        start = (number // 3) * PAD * PAD + (number % 3) * PAD
        columns[number * C : (number + 1) * C, 0:length] = source[:, start : start + length]


def three_taps(weight, columns, length):
    parts = jnp.dot(weight[...], columns[:, 0:length], preferred_element_type=F32)
    return (
        parts[0:C]
        + pltpu.roll(parts[C : 2 * C], length - 1, 1)
        + pltpu.roll(parts[2 * C :], length - 2, 1)
    )


def weight_grad(gradient, columns, grads, tiles):
    stack = jnp.concatenate(
        [gradient, pltpu.roll(gradient, 1, 1), pltpu.roll(gradient, 2, 1)], axis=0
    ).astype(BF16)
    sums = lax.dot_general(
        stack, columns, (((1,), (1,)), ((), ())), preferred_element_type=F32
    ) * (1.0 / 512.0)
    for number in range(9):
        for dz in range(3):
            k = number * 3 + dz
            grads[:, k * C : (k + 1) * C] = sums[
                dz * C : (dz + 1) * C, number * C : (number + 1) * C
            ]
    grads[:, 27 * C :] = jnp.zeros((C, TILES_L * 128 - 27 * C), F32)
    for tile in range(6 * TILES_L):
        row, lane = tile // TILES_L * 16, tile % TILES_L * 128
        tiles[tile] = grads[row : row + 16, lane : lane + 128]
    tiles[6 * TILES_L :] = jnp.zeros((128 - 6 * TILES_L, 16, 128), F32)


def relative_owners(adj, own):
    owners = [adj[0, k] for k in range(27)]
    return [jnp.where(block < 0, 99, block // REPS - own[0]) for block in owners]


def among(relative, steps):
    found = relative[0] == steps[0]
    for value in relative:
        for step in steps:
            found = jnp.logical_or(found, value == step)
    return found


def prepare_kernel(
    adj, own, first_in, second_in, first_forward, second_turned, places, low, side,
    first, second, sems,
):
    copies = start_weights(first_in, second_in, first, second, sems)
    relative = relative_owners(adj, own)
    from_left = among(relative, [-1 - GRID, -1, -1 + GRID])
    side[...] = jnp.full(side.shape, jnp.where(from_left, 1.0, 0.0), F32).astype(BF16)
    from_low = among(relative, [-GRID])
    low[...] = jnp.full(low.shape, jnp.where(from_low, 1.0, 0.0), F32).astype(BF16)
    p = ints((1, LANES), 1)
    at = [p // (PAD * PAD) - 2, p // PAD % PAD - 2, p % PAD - 2]
    out = [jnp.where(v < 0, 0, jnp.where(v >= BE, 2, 1)) for v in at]
    site = jnp.where(p < PAD**3, out[0] * 9 + out[1] * 3 + out[2], 27)
    x, y, z = (jnp.where(v < 0, v + BE, jnp.where(v >= BE, v - BE, v)) for v in at)
    which = jnp.full((1, LANES), 99, jnp.int32)
    for k in range(27):
        which = jnp.where(site == k, relative[k], which)
    place = jnp.where(which == 0, x * 64 + y * 8 + z, -1)
    for sx, sy in DIRECTIONS:
        nx, ny = (x - 6 if sx < 0 else x), (y - 6 if sy < 0 else y)
        if sx == 0:
            there = 512 + x * 16 + ny * 8 + z
        elif sy == 0:
            there = 640 + nx * 64 + y * 8 + z
        else:
            there = (768 if sy < 0 else 800) + nx * 16 + ny * 8 + z
        place = jnp.where(which == sx + GRID * sy, there, place)
    places[...] = jnp.broadcast_to(place, places.shape)
    copies[0].wait()
    forward_weight(first, first_forward)
    copies[1].wait()
    turned_weight(second, second_turned)


def either(flag, one, other):
    return one * flag + other * (1.0 - flag.astype(F32)).astype(BF16)


def place_kernel(q0, q1, q2, q3, ym, yp, places, low, base, hot_x, sources):
    for number, quarter in enumerate((q0, q1, q2, q3)):
        sources[:, number * 128 : (number + 1) * 128] = quarter[...]
    sources[:, 512:640] = either(low[0:1, :], ym[...], yp[...])
    width = 384
    for part in range(LANES // width):
        cut = slice(part * width, (part + 1) * width)
        hot = jnp.where(ints((896, width), 0) == places[0:1, cut], 1.0, 0.0).astype(BF16)
        hot_x[:, cut] = hot[640:896]
        base[:, cut] = jnp.dot(
            sources[...], hot[0:640], preferred_element_type=F32
        ).astype(BF16)


def main_kernel(
    own, xm, xp, base, hot_x, side, w_one, w_two,
    send, padded, hidden, grad_one, inner, columns,
    col_g, grads,
):
    slab = either(side[0:1, :], xm[...], xp[...])
    width = 384
    for part in range(LANES // width):
        cut = slice(part * width, (part + 1) * width)
        near = jnp.dot(slab, hot_x[:, cut], preferred_element_type=F32)
        padded[:, cut] = (base[:, cut].astype(F32) + near).astype(BF16)
    shifted_columns(padded[0:C, :], columns.at[0], OUTER)
    shifted_columns(padded[C : 2 * C, :], col_g, OUTER)
    mask = padded[2 * C : 2 * C + 1, BASE + 1 : BASE + 1 + OUTER].astype(F32)
    pre = three_taps(w_one, columns.at[0], OUTER)
    sig = jax.nn.sigmoid(pre)
    hidden[...] = (pre * sig * mask).astype(BF16)
    back = three_taps(w_two, col_g, OUTER)
    grad = (back * mask * sig * (1.0 + pre * (1.0 - sig))).astype(BF16)
    grad_one[...] = grad
    shifted_columns(hidden[...], columns.at[1], INNER)
    columns[1, :, INNER:OUTER] = jnp.zeros((9 * C, OUTER - INNER), BF16)
    kept = jnp.where(own_voxels(BASE + 1, OUTER), 1.0, 0.0)
    inner[0] = (grad.astype(F32) * kept).astype(BF16)
    start = 2 * (BASE + 1)
    kept = jnp.where(own_voxels(start, INNER), 1.0, 0.0)
    grad_two = padded[C : 2 * C, start : start + INNER].astype(F32)
    inner[1, :, 0:INNER] = (grad_two * kept).astype(BF16)
    inner[1, :, INNER:OUTER] = jnp.zeros((C, OUTER - INNER), BF16)
    weight_grad(inner[1 - own[1]].astype(F32), columns[1 - own[1]], grads, send)


def keep_kernel(own, inner, columns, keep, grads):
    weight_grad(inner[own[1]].astype(F32), columns[own[1]], grads, keep)


def out_kernel(after, padded, hidden, grad_one, w_two, w_one, out_feats, grad_feats, done, columns):
    done[...] = jnp.zeros((8, 128), F32)
    voxel = ints((INNER, 512), 1)
    inner = voxel // 64 * (PAD * PAD) + voxel // 8 % 8 * PAD + voxel % 8
    squeeze = jnp.where(ints((INNER, 512), 0) == inner, 1.0, 0.0).astype(BF16)
    start = 2 * (BASE + 1)
    mask = padded[2 * C : 2 * C + 1, start : start + INNER].astype(F32)
    for first, field, weight, out in (
        (0, hidden, w_two, out_feats),
        (C, grad_one, w_one, grad_feats),
    ):
        shifted_columns(field[...], columns, INNER)
        pre = three_taps(weight, columns, INNER)
        kept = padded[first : first + C, start : start + INNER].astype(F32)
        wide = (kept + pre * mask).astype(BF16)
        out[0] = jnp.dot(wide, squeeze, preferred_element_type=F32).astype(BF16)


def pair_kernel(keep, other, coded):
    for number in range(32):
        tiles = slice(number * 4, number * 4 + 4)
        total = keep[tiles] + other[tiles]
        most = jnp.maximum(jnp.max(jnp.abs(total), axis=1), 1e-30)
        exponent = jnp.ceil(jnp.log2(most))
        values = jnp.round(total * jnp.exp2(14.0 - exponent)[:, None, :])
        coded[number, 0:4] = values.astype(jnp.int32).astype(jnp.int16)
        rows = jnp.concatenate([exponent, jnp.zeros((12, 128), F32)], axis=0)
        coded[number, 4] = rows.astype(jnp.int32).astype(jnp.int16)


def decode_kernel(coded, copies):
    total = jnp.zeros((4, 16, 128), F32)
    for number in range(32):
        exponent = coded[number, 4].astype(jnp.int32).astype(F32)[0:4]
        values = coded[number, 0:4].astype(jnp.int32).astype(F32)
        total = total + values * jnp.exp2(exponent - 14.0)[:, None, :]
    for number in range(copies.shape[0]):
        copies[number] = total.astype(BF16)


def share_kernel(count, parts, *refs):
    total = parts[0].astype(F32)
    for number in range(1, count):
        total = total + parts[number].astype(F32)
    copies = refs[-1]
    for number in range(copies.shape[0]):
        copies[number] = total.astype(BF16)


def write_half(half, out, rows, sems):
    copies = []
    for row in range(6):
        for lane in range(TILES_L):
            last = min((lane + 1) * 128, 27 * C)
            part = half[row * TILES_L + lane].astype(F32)
            rows[row * 16 : row * 16 + 16, lane * 128 : last] = part[:, : last - lane * 128]
        at = pl.ds(row * 16, 16)
        copies.append(pltpu.make_async_copy(rows.at[at], out.at[at], sems.at[row]))
        copies[-1].start()
    for copy in copies:
        copy.wait()


def mine_kernel(own, half, first, second, rows, sems):
    @pl.when(own[1] == 0)
    def _():
        write_half(half, first, rows, sems)

    @pl.when(own[1] != 0)
    def _():
        write_half(half, second, rows, sems)


def other_kernel(own, half, first_in, second_in, first, second, rows, sems):
    @pl.when(own[1] == 0)
    def _():
        write_half(half, second, rows, sems)

    @pl.when(own[1] != 0)
    def _():
        write_half(half, first, rows, sems)


VMEM = pl.BlockSpec(memory_space=pltpu.VMEM)
SMEM = pl.BlockSpec(memory_space=pltpu.SMEM)
HBM = pl.BlockSpec(memory_space=pltpu.HBM)
ANY = pl.BlockSpec(memory_space=pl.ANY)
DMA = pltpu.SemaphoreType.DMA
MIB = 1024 * 1024
PACK, PREPARE, LATE = int(53.58 * MIB), int(52.4 * MIB), int(52.5 * MIB)


def call(kernel, outs, specs, scratch=(), place=VMEM, limit=40 * MIB, **options):
    return pl.pallas_call(
        kernel,
        out_shape=[jax.ShapeDtypeStruct(*out) for out in outs],
        in_specs=specs,
        out_specs=[place] * len(outs),
        scratch_shapes=scratch,
        compiler_params=pltpu.CompilerParams(vmem_limit_bytes=limit),
        **options,
    )


def from_owner(value, sx, sy):
    pairs = []
    for owner in range(GRID * GRID):
        column, row = owner % GRID + sx, owner // GRID + sy
        if 0 <= column < GRID and 0 <= row < GRID:
            pairs.append((row * GRID + column, owner))
    return lax.ppermute(value, ("zh", "zl", "y"), pairs)


def swap_halves(value):
    return lax.ppermute(value, "core", [(0, 1), (1, 0)])


def body(feats, cotangent, occupancy, counts, adjacency, w_first, w_second):
    own = jnp.stack([lax.axis_index(("zh", "zl", "y")), lax.axis_index("core")]).astype(jnp.int32)
    rim, slab, turned = ((ROWS, 128), BF16), ((ROWS, 256), BF16), ((3 * C, 9 * C), BF16)
    vmem = pltpu.VMEM
    inputs = [
        vmem((1, C, 512), BF16), vmem((1, C, 512), BF16), vmem((1, 512), jnp.int32), DMA((3,))
    ]
    weights = [vmem((C, 27 * C), BF16)] * 2 + [DMA((2,))]
    with jax.named_scope("pack"):
        down, up, *quarters = call(
            pack_kernel, [rim] * 6, [HBM] * 3, [vmem((ROWS, 512), BF16)] + inputs, limit=PACK
        )(feats, cotangent, occupancy)
    with jax.named_scope("prepare"):
        one_f, two_b, places, low, side = call(
            prepare_kernel,
            [turned] * 2
            + [((8, LANES), jnp.int32), ((16, 128), BF16), ((16, 256), BF16)],
            [SMEM] * 2 + [HBM] * 2,
            weights,
            limit=PREPARE,
        )(adjacency, own, w_first, w_second)
    with jax.named_scope("rims_y"):
        ym, yp = from_owner(down, 0, -1), from_owner(up, 0, 1)
    with jax.named_scope("slabs"):
        left, right = call(slab_kernel, [slab, slab], [VMEM] * 5)(
            side, quarters[0], quarters[3], ym, yp
        )
    with jax.named_scope("rims_x"):
        xm, xp = from_owner(left, -1, 0), from_owner(right, 1, 0)
    with jax.named_scope("place"):
        base, hot_x = call(
            place_kernel,
            [((ROWS, LANES), BF16), ((256, LANES), BF16)],
            [VMEM] * 8,
            [vmem((ROWS, 640), BF16)],
        )(*quarters, ym, yp, places, low)
    half, grads = ((128, 16, 128), F32), vmem((C, TILES_L * 128), F32)
    outer = ((C, OUTER), BF16)
    with jax.named_scope("middle"):
        send, padded, hidden, grad_one, inner, columns = call(
            main_kernel,
            [
                half, ((ROWS, LANES), BF16), outer, outer,
                ((2, C, OUTER), BF16), ((2, 9 * C, OUTER), BF16),
            ],
            [SMEM] + [VMEM] * 7,
            [vmem((9 * C, OUTER), BF16), grads],
        )(own, xm, xp, base, hot_x, side, one_f, two_b)
    with jax.named_scope("keep"):
        (keep,) = call(keep_kernel, [half], [SMEM] + [VMEM] * 2, [grads])(own, inner, columns)
    with jax.named_scope("pair"):
        (coded,) = call(pair_kernel, [((32, 5, 16, 128), jnp.int16)], [VMEM] * 2)(
            keep, swap_halves(send)
        )
    near, far = ("zl", "y", "x"), "zh"
    with jax.named_scope("sum"):
        parts = lax.all_to_all(coded, near, 0, 0)
        (copies,) = call(decode_kernel, [((8, 4, 16, 128), BF16)], [VMEM])(parts)
        parts = lax.all_to_all(copies, far, 0, 0)
    with jax.named_scope("late_weights"):
        two_f, one_b = call(
            late_weight_kernel, [turned] * 2, [ANY] + [HBM] * 2, weights, limit=LATE
        )(copies, w_first, w_second)
    with jax.named_scope("outputs"):
        out_feats, grad_feats, done = call(
            out_kernel,
            [((1, C, 512), BF16)] * 2 + [((8, 128), F32)],
            [ANY] + [VMEM] * 5,
            [vmem((9 * C, INNER), BF16)],
        )(copies, padded, hidden, grad_one, two_f, one_b)
    with jax.named_scope("shares"):
        (copies,) = call(
            lambda *refs: share_kernel(8, *refs), [((32, 4, 16, 128), BF16)], [VMEM] * 2
        )(parts, done)
        mine = lax.all_to_all(copies, near, 0, 0).reshape(128, 16, 128)
        other = swap_halves(mine)
    grad, rows = ((C, 27 * C), F32), [vmem((C, 27 * C), F32), DMA((6,))]
    with jax.named_scope("mine"):
        begun = call(mine_kernel, [grad] * 2, [SMEM, VMEM], rows, place=ANY)(own, mine)
    with jax.named_scope("other"):
        grad_first, grad_second = call(
            other_kernel, [grad] * 2, [SMEM, VMEM, ANY, ANY], rows, place=ANY,
            input_output_aliases={2: 0, 3: 1},
        )(own, other, *begun)
    return out_feats, grad_feats, grad_first, grad_second


def solution(mesh):
    fine = Mesh(mesh.devices.reshape(8, 2, 4, 4, 2), ("zh", "zl", "y", "x", "core"))
    both = ("zh", "zl", "y", "x", "core")
    blocks = P(both, None, None)
    rows = P(both, None)
    return jax.shard_map(
        body,
        mesh=fine,
        in_specs=(blocks, blocks, rows, rows, rows, P(), P()),
        out_specs=(blocks, blocks, P(), P()),
        check_vma=False,
    )
```

```python
import jax
import jax.numpy as jnp
import numpy as np
from jax import lax
from jax.experimental import pallas as pl
from jax.experimental.pallas import tpu as pltpu
from jax.sharding import Mesh, PartitionSpec as P

C = 96
BE = 8
GRID = 8
REPS = 8
ROWS = 208
PAD = 12
LANES = 1920
OUTER = 1536
INNER = 1152
BASE = PAD * PAD + PAD
TILES_L = 21
DIRECTIONS = [(-1, -1), (0, -1), (1, -1), (-1, 0), (1, 0), (-1, 1), (0, 1), (1, 1)]
OFFSETS = [(a, b, c) for a in (-1, 0, 1) for b in (-1, 0, 1) for c in (-1, 0, 1)]
F32, BF16 = jnp.float32, jnp.bfloat16


def ints(dims, axis):
    return lax.broadcasted_iota(jnp.int32, dims, axis)


def own_voxels(first, length):
    p = ints((1, length), 1) + first
    x, y, z = p // (PAD * PAD), p // PAD % PAD, p % PAD
    inside = [jnp.logical_and(at >= 2, at < 10) for at in (x, y, z)]
    return jnp.logical_and(jnp.logical_and(inside[0], inside[1]), inside[2])


def start_inputs(feats_in, cot_in, occ_in, feats, cot, occ, sems):
    copies = [
        pltpu.make_async_copy(source, target, sems.at[number])
        for number, (source, target) in enumerate(((occ_in, occ), (feats_in, feats), (cot_in, cot)))
    ]
    for copy in copies:
        copy.start()
    return copies


def mask_inputs(copies, feats, cot, occ, field):
    copies[0].wait()
    mask = (occ[...] != 0).astype(F32).astype(BF16)
    field[2 * C :, 0:512] = jnp.broadcast_to(mask, (ROWS - 2 * C, 512))
    copies[1].wait()
    field[0:C, 0:512] = feats[0] * mask
    copies[2].wait()
    field[C : 2 * C, 0:512] = cot[0] * mask


def pack_kernel(feats_in, cot_in, occ_in, down, up, *refs):
    quarters, (field, feats, cot, occ, sems) = refs[:4], refs[4:]
    copies = start_inputs(feats_in, cot_in, occ_in, feats, cot, occ, sems)
    lane = ints((512, 256), 1)
    rim = lane % 128
    wanted = rim // 16 * 64 + rim // 8 % 2 * 8 + rim % 8 + jnp.where(lane < 128, 48, 0)
    picks = jnp.where(ints((512, 256), 0) == wanted, 1.0, 0.0).astype(BF16)
    mask_inputs(copies, feats, cot, occ, field)
    rims = jnp.dot(field[...], picks, preferred_element_type=F32).astype(BF16)
    down[...] = rims[:, 0:128]
    up[...] = rims[:, 128:256]
    for number in range(4):
        quarters[number][...] = field[:, number * 128 : (number + 1) * 128]


def slab_kernel(after, first, last, ym, yp, left, right):
    blank = jnp.zeros((ROWS, 64), BF16)
    left[:, 0:128] = last[...]
    left[:, 128:256] = jnp.concatenate([ym[:, 96:128], yp[:, 96:128], blank], axis=1)
    right[:, 0:128] = first[...]
    right[:, 128:256] = jnp.concatenate([ym[:, 0:32], yp[:, 0:32], blank], axis=1)


def tap_blocks():
    for number in range(9):
        for dz in range(3):
            k = number * 3 + dz
            yield k, slice(dz * C, (dz + 1) * C), slice(number * C, (number + 1) * C)


def forward_weight(weight, out):
    whole = weight[...]
    for k, rows, columns in tap_blocks():
        out[rows, columns] = whole[:, k * C : (k + 1) * C]


def turned_weight(weight, out):
    across = weight[...].astype(F32).T.astype(BF16)
    for k, rows, columns in tap_blocks():
        out[rows, columns] = across[(26 - k) * C : (27 - k) * C, :]


def start_weights(first_in, second_in, first, second, sems):
    copies = [
        pltpu.make_async_copy(first_in, first, sems.at[0]),
        pltpu.make_async_copy(second_in, second, sems.at[1]),
    ]
    for copy in copies:
        copy.start()
    return copies


def late_weight_kernel(after, first_in, second_in, second_forward, first_turned, first, second, sems):
    copies = start_weights(first_in, second_in, first, second, sems)
    copies[1].wait()
    forward_weight(second, second_forward)
    copies[0].wait()
    turned_weight(first, first_turned)


def shifted_columns(source, columns, length):
    for number in range(9):
        start = (number // 3) * PAD * PAD + (number % 3) * PAD
        columns[number * C : (number + 1) * C, 0:length] = source[:, start : start + length]


def three_taps(weight, columns, length):
    parts = jnp.dot(weight[...], columns[:, 0:length], preferred_element_type=F32)
    return (
        parts[0:C]
        + pltpu.roll(parts[C : 2 * C], length - 1, 1)
        + pltpu.roll(parts[2 * C :], length - 2, 1)
    )


def weight_grad(gradient, columns, grads, tiles):
    stack = jnp.concatenate(
        [gradient, pltpu.roll(gradient, 1, 1), pltpu.roll(gradient, 2, 1)], axis=0
    ).astype(BF16)
    sums = lax.dot_general(
        stack, columns, (((1,), (1,)), ((), ())), preferred_element_type=F32
    ) * (1.0 / 512.0)
    for number in range(9):
        for dz in range(3):
            k = number * 3 + dz
            grads[:, k * C : (k + 1) * C] = sums[
                dz * C : (dz + 1) * C, number * C : (number + 1) * C
            ]
    grads[:, 27 * C :] = jnp.zeros((C, TILES_L * 128 - 27 * C), F32)
    for tile in range(6 * TILES_L):
        row, lane = tile // TILES_L * 16, tile % TILES_L * 128
        tiles[tile] = grads[row : row + 16, lane : lane + 128]
    tiles[6 * TILES_L :] = jnp.zeros((128 - 6 * TILES_L, 16, 128), F32)


def relative_owners(adj, own):
    owners = [adj[0, k] for k in range(27)]
    return [jnp.where(block < 0, 99, block // REPS - own[0]) for block in owners]


def among(relative, steps):
    found = relative[0] == steps[0]
    for value in relative:
        for step in steps:
            found = jnp.logical_or(found, value == step)
    return found


def prepare_kernel(
    adj, own, first_in, second_in, first_forward, second_turned, places, low, side,
    first, second, sems,
):
    copies = start_weights(first_in, second_in, first, second, sems)
    relative = relative_owners(adj, own)
    from_left = among(relative, [-1 - GRID, -1, -1 + GRID])
    side[...] = jnp.full(side.shape, jnp.where(from_left, 1.0, 0.0), F32).astype(BF16)
    from_low = among(relative, [-GRID])
    low[...] = jnp.full(low.shape, jnp.where(from_low, 1.0, 0.0), F32).astype(BF16)
    p = ints((1, LANES), 1)
    at = [p // (PAD * PAD) - 2, p // PAD % PAD - 2, p % PAD - 2]
    out = [jnp.where(v < 0, 0, jnp.where(v >= BE, 2, 1)) for v in at]
    site = jnp.where(p < PAD**3, out[0] * 9 + out[1] * 3 + out[2], 27)
    x, y, z = (jnp.where(v < 0, v + BE, jnp.where(v >= BE, v - BE, v)) for v in at)
    which = jnp.full((1, LANES), 99, jnp.int32)
    for k in range(27):
        which = jnp.where(site == k, relative[k], which)
    place = jnp.where(which == 0, x * 64 + y * 8 + z, -1)
    for sx, sy in DIRECTIONS:
        nx, ny = (x - 6 if sx < 0 else x), (y - 6 if sy < 0 else y)
        if sx == 0:
            there = 512 + x * 16 + ny * 8 + z
        elif sy == 0:
            there = 640 + nx * 64 + y * 8 + z
        else:
            there = (768 if sy < 0 else 800) + nx * 16 + ny * 8 + z
        place = jnp.where(which == sx + GRID * sy, there, place)
    places[...] = jnp.broadcast_to(place, places.shape)
    copies[0].wait()
    forward_weight(first, first_forward)
    copies[1].wait()
    turned_weight(second, second_turned)


def either(flag, one, other):
    return one * flag + other * (1.0 - flag.astype(F32)).astype(BF16)


def place_kernel(q0, q1, q2, q3, ym, yp, places, low, base, hot_x, sources):
    for number, quarter in enumerate((q0, q1, q2, q3)):
        sources[:, number * 128 : (number + 1) * 128] = quarter[...]
    sources[:, 512:640] = either(low[0:1, :], ym[...], yp[...])
    width = 384
    for part in range(LANES // width):
        cut = slice(part * width, (part + 1) * width)
        hot = jnp.where(ints((896, width), 0) == places[0:1, cut], 1.0, 0.0).astype(BF16)
        hot_x[:, cut] = hot[640:896]
        base[:, cut] = jnp.dot(
            sources[...], hot[0:640], preferred_element_type=F32
        ).astype(BF16)


def main_kernel(
    own, xm, xp, base, hot_x, side, w_one, w_two,
    send, padded, hidden, grad_one, inner, columns,
    col_g, grads,
):
    slab = either(side[0:1, :], xm[...], xp[...])
    width = 384
    for part in range(LANES // width):
        cut = slice(part * width, (part + 1) * width)
        near = jnp.dot(slab, hot_x[:, cut], preferred_element_type=F32)
        padded[:, cut] = (base[:, cut].astype(F32) + near).astype(BF16)
    shifted_columns(padded[0:C, :], columns.at[0], OUTER)
    shifted_columns(padded[C : 2 * C, :], col_g, OUTER)
    mask = padded[2 * C : 2 * C + 1, BASE + 1 : BASE + 1 + OUTER].astype(F32)
    pre = three_taps(w_one, columns.at[0], OUTER)
    sig = jax.nn.sigmoid(pre)
    hidden[...] = (pre * sig * mask).astype(BF16)
    back = three_taps(w_two, col_g, OUTER)
    grad = (back * mask * sig * (1.0 + pre * (1.0 - sig))).astype(BF16)
    grad_one[...] = grad
    shifted_columns(hidden[...], columns.at[1], INNER)
    columns[1, :, INNER:OUTER] = jnp.zeros((9 * C, OUTER - INNER), BF16)
    kept = jnp.where(own_voxels(BASE + 1, OUTER), 1.0, 0.0)
    inner[0] = (grad.astype(F32) * kept).astype(BF16)
    start = 2 * (BASE + 1)
    kept = jnp.where(own_voxels(start, INNER), 1.0, 0.0)
    grad_two = padded[C : 2 * C, start : start + INNER].astype(F32)
    inner[1, :, 0:INNER] = (grad_two * kept).astype(BF16)
    inner[1, :, INNER:OUTER] = jnp.zeros((C, OUTER - INNER), BF16)
    weight_grad(inner[1 - own[1]].astype(F32), columns[1 - own[1]], grads, send)


def keep_kernel(own, inner, columns, keep, grads):
    weight_grad(inner[own[1]].astype(F32), columns[own[1]], grads, keep)


def out_kernel(after, padded, hidden, grad_one, w_two, w_one, out_feats, grad_feats, done, columns):
    done[...] = jnp.zeros((8, 128), F32)
    voxel = ints((INNER, 512), 1)
    inner = voxel // 64 * (PAD * PAD) + voxel // 8 % 8 * PAD + voxel % 8
    squeeze = jnp.where(ints((INNER, 512), 0) == inner, 1.0, 0.0).astype(BF16)
    start = 2 * (BASE + 1)
    mask = padded[2 * C : 2 * C + 1, start : start + INNER].astype(F32)
    for first, field, weight, out in (
        (0, hidden, w_two, out_feats),
        (C, grad_one, w_one, grad_feats),
    ):
        shifted_columns(field[...], columns, INNER)
        pre = three_taps(weight, columns, INNER)
        kept = padded[first : first + C, start : start + INNER].astype(F32)
        wide = (kept + pre * mask).astype(BF16)
        out[0] = jnp.dot(wide, squeeze, preferred_element_type=F32).astype(BF16)


def power_of_two(exponent):
    power = jnp.ones(exponent.shape, F32)
    for sign in (1.0, -1.0):
        rest = jnp.maximum(exponent * sign, 0.0)
        for bit in (64.0, 32.0, 16.0, 8.0, 4.0, 2.0, 1.0):
            has = rest >= bit
            power = jnp.where(has, power * 2.0 ** (sign * bit), power)
            rest = jnp.where(has, rest - bit, rest)
    return power


def pair_kernel(keep, other, coded):
    for number in range(32):
        tiles = slice(number * 4, number * 4 + 4)
        total = keep[tiles] + other[tiles]
        most = jnp.maximum(jnp.max(jnp.abs(total), axis=1), 1e-30)
        exponent = jnp.ceil(jnp.log2(most))
        values = jnp.round(total * power_of_two(14.0 - exponent)[:, None, :])
        coded[number, 0:64] = values.astype(jnp.int32).astype(jnp.int16).reshape(64, 128)
        rows = jnp.concatenate([exponent, jnp.zeros((4, 128), F32)], axis=0)
        coded[number, 64:72] = rows.astype(jnp.int32).astype(jnp.int16)


def decode_kernel(coded, copies):
    total = jnp.zeros((4, 16, 128), F32)
    for number in range(32):
        exponent = coded[number, 64:72].astype(jnp.int32).astype(F32)[0:4]
        values = coded[number, 0:64].astype(jnp.int32).astype(F32).reshape(4, 16, 128)
        total = total + values * power_of_two(exponent - 14.0)[:, None, :]
    for number in range(copies.shape[0]):
        copies[number] = total.astype(BF16)


def share_kernel(count, parts, *refs):
    total = parts[0].astype(F32)
    for number in range(1, count):
        total = total + parts[number].astype(F32)
    copies = refs[-1]
    for number in range(copies.shape[0]):
        copies[number] = total.astype(BF16)


def write_half(half, out, rows, sems):
    copies = []
    for row in range(6):
        for lane in range(TILES_L):
            last = min((lane + 1) * 128, 27 * C)
            part = half[row * TILES_L + lane].astype(F32)
            rows[row * 16 : row * 16 + 16, lane * 128 : last] = part[:, : last - lane * 128]
        at = pl.ds(row * 16, 16)
        copies.append(pltpu.make_async_copy(rows.at[at], out.at[at], sems.at[row]))
        copies[-1].start()
    for copy in copies:
        copy.wait()


def mine_kernel(own, half, first, second, rows, sems):
    @pl.when(own[1] == 0)
    def _():
        write_half(half, first, rows, sems)

    @pl.when(own[1] != 0)
    def _():
        write_half(half, second, rows, sems)


def other_kernel(own, half, first_in, second_in, first, second, rows, sems):
    @pl.when(own[1] == 0)
    def _():
        write_half(half, second, rows, sems)

    @pl.when(own[1] != 0)
    def _():
        write_half(half, first, rows, sems)


VMEM = pl.BlockSpec(memory_space=pltpu.VMEM)
SMEM = pl.BlockSpec(memory_space=pltpu.SMEM)
HBM = pl.BlockSpec(memory_space=pltpu.HBM)
ANY = pl.BlockSpec(memory_space=pl.ANY)
DMA = pltpu.SemaphoreType.DMA
MIB = 1024 * 1024
PACK, PREPARE, LATE = int(53.58 * MIB), int(52.4 * MIB), int(52.5 * MIB)


def call(kernel, outs, specs, scratch=(), place=VMEM, limit=40 * MIB, **options):
    return pl.pallas_call(
        kernel,
        out_shape=[jax.ShapeDtypeStruct(*out) for out in outs],
        in_specs=specs,
        out_specs=[place] * len(outs),
        scratch_shapes=scratch,
        compiler_params=pltpu.CompilerParams(vmem_limit_bytes=limit),
        **options,
    )


def from_owner(value, sx, sy):
    pairs = []
    for owner in range(GRID * GRID):
        column, row = owner % GRID + sx, owner // GRID + sy
        if 0 <= column < GRID and 0 <= row < GRID:
            pairs.append((row * GRID + column, owner))
    return lax.ppermute(value, ("zh", "zl", "y"), pairs)


def swap_halves(value):
    return lax.ppermute(value, "core", [(0, 1), (1, 0)])


def body(feats, cotangent, occupancy, counts, adjacency, w_first, w_second):
    own = jnp.stack([lax.axis_index(("zh", "zl", "y")), lax.axis_index("core")]).astype(jnp.int32)
    rim, slab, turned = ((ROWS, 128), BF16), ((ROWS, 256), BF16), ((3 * C, 9 * C), BF16)
    vmem = pltpu.VMEM
    inputs = [
        vmem((1, C, 512), BF16), vmem((1, C, 512), BF16), vmem((1, 512), jnp.int32), DMA((3,))
    ]
    weights = [vmem((C, 27 * C), BF16)] * 2 + [DMA((2,))]
    with jax.named_scope("pack"):
        down, up, *quarters = call(
            pack_kernel, [rim] * 6, [HBM] * 3, [vmem((ROWS, 512), BF16)] + inputs, limit=PACK
        )(feats, cotangent, occupancy)
    with jax.named_scope("prepare"):
        one_f, two_b, places, low, side = call(
            prepare_kernel,
            [turned] * 2
            + [((8, LANES), jnp.int32), ((16, 128), BF16), ((16, 256), BF16)],
            [SMEM] * 2 + [HBM] * 2,
            weights,
            limit=PREPARE,
        )(adjacency, own, w_first, w_second)
    with jax.named_scope("rims_y"):
        ym, yp = from_owner(down, 0, -1), from_owner(up, 0, 1)
    with jax.named_scope("slabs"):
        left, right = call(slab_kernel, [slab, slab], [VMEM] * 5)(
            side, quarters[0], quarters[3], ym, yp
        )
    with jax.named_scope("rims_x"):
        xm, xp = from_owner(left, -1, 0), from_owner(right, 1, 0)
    with jax.named_scope("place"):
        base, hot_x = call(
            place_kernel,
            [((ROWS, LANES), BF16), ((256, LANES), BF16)],
            [VMEM] * 8,
            [vmem((ROWS, 640), BF16)],
        )(*quarters, ym, yp, places, low)
    half, grads = ((128, 16, 128), F32), vmem((C, TILES_L * 128), F32)
    outer = ((C, OUTER), BF16)
    with jax.named_scope("middle"):
        send, padded, hidden, grad_one, inner, columns = call(
            main_kernel,
            [
                half, ((ROWS, LANES), BF16), outer, outer,
                ((2, C, OUTER), BF16), ((2, 9 * C, OUTER), BF16),
            ],
            [SMEM] + [VMEM] * 7,
            [vmem((9 * C, OUTER), BF16), grads],
        )(own, xm, xp, base, hot_x, side, one_f, two_b)
    with jax.named_scope("keep"):
        (keep,) = call(keep_kernel, [half], [SMEM] + [VMEM] * 2, [grads])(own, inner, columns)
    with jax.named_scope("pair"):
        (coded,) = call(pair_kernel, [((32, 72, 128), jnp.int16)], [VMEM] * 2)(
            keep, swap_halves(send)
        )
    near, far = ("zl", "y", "x"), "zh"
    with jax.named_scope("sum"):
        parts = lax.all_to_all(coded, near, 0, 0)
        (copies,) = call(decode_kernel, [((8, 4, 16, 128), BF16)], [VMEM])(parts)
        parts = lax.all_to_all(copies, far, 0, 0)
    with jax.named_scope("late_weights"):
        two_f, one_b = call(
            late_weight_kernel, [turned] * 2, [ANY] + [HBM] * 2, weights, limit=LATE
        )(copies, w_first, w_second)
    with jax.named_scope("outputs"):
        out_feats, grad_feats, done = call(
            out_kernel,
            [((1, C, 512), BF16)] * 2 + [((8, 128), F32)],
            [ANY] + [VMEM] * 5,
            [vmem((9 * C, INNER), BF16)],
        )(copies, padded, hidden, grad_one, two_f, one_b)
    with jax.named_scope("shares"):
        (copies,) = call(
            lambda *refs: share_kernel(8, *refs), [((32, 4, 16, 128), BF16)], [VMEM] * 2
        )(parts, done)
        mine = lax.all_to_all(copies, near, 0, 0).reshape(128, 16, 128)
        other = swap_halves(mine)
    grad, rows = ((C, 27 * C), F32), [vmem((C, 27 * C), F32), DMA((6,))]
    with jax.named_scope("mine"):
        begun = call(mine_kernel, [grad] * 2, [SMEM, VMEM], rows, place=ANY)(own, mine)
    with jax.named_scope("other"):
        grad_first, grad_second = call(
            other_kernel, [grad] * 2, [SMEM, VMEM, ANY, ANY], rows, place=ANY,
            input_output_aliases={2: 0, 3: 1},
        )(own, other, *begun)
    return out_feats, grad_feats, grad_first, grad_second


def solution(mesh):
    fine = Mesh(mesh.devices.reshape(8, 2, 4, 4, 2), ("zh", "zl", "y", "x", "core"))
    both = ("zh", "zl", "y", "x", "core")
    blocks = P(both, None, None)
    rows = P(both, None)
    return jax.shard_map(
        body,
        mesh=fine,
        in_specs=(blocks, blocks, rows, rows, rows, P(), P()),
        out_specs=(blocks, blocks, P(), P()),
        check_vma=False,
    )
```

```python
import jax
import jax.numpy as jnp
import numpy as np
from jax import lax
from jax.experimental import pallas as pl
from jax.experimental.pallas import tpu as pltpu
from jax.sharding import Mesh, PartitionSpec as P

C = 96
BE = 8
GRID = 8
REPS = 8
ROWS = 208
PAD = 12
LANES = 1920
OUTER = 1536
INNER = 1152
BASE = PAD * PAD + PAD
TILES_L = 21
DIRECTIONS = [(-1, -1), (0, -1), (1, -1), (-1, 0), (1, 0), (-1, 1), (0, 1), (1, 1)]
OFFSETS = [(a, b, c) for a in (-1, 0, 1) for b in (-1, 0, 1) for c in (-1, 0, 1)]
F32, BF16 = jnp.float32, jnp.bfloat16


def ints(dims, axis):
    return lax.broadcasted_iota(jnp.int32, dims, axis)


def own_voxels(first, length):
    p = ints((1, length), 1) + first
    x, y, z = p // (PAD * PAD), p // PAD % PAD, p % PAD
    inside = [jnp.logical_and(at >= 2, at < 10) for at in (x, y, z)]
    return jnp.logical_and(jnp.logical_and(inside[0], inside[1]), inside[2])


def start_inputs(feats_in, cot_in, occ_in, feats, cot, occ, sems):
    copies = [
        pltpu.make_async_copy(source, target, sems.at[number])
        for number, (source, target) in enumerate(((occ_in, occ), (feats_in, feats), (cot_in, cot)))
    ]
    for copy in copies:
        copy.start()
    return copies


def mask_inputs(copies, feats, cot, occ, field):
    copies[0].wait()
    mask = (occ[...] != 0).astype(F32).astype(BF16)
    field[2 * C :, 0:512] = jnp.broadcast_to(mask, (ROWS - 2 * C, 512))
    copies[1].wait()
    field[0:C, 0:512] = feats[0] * mask
    copies[2].wait()
    field[C : 2 * C, 0:512] = cot[0] * mask


def pack_kernel(feats_in, cot_in, occ_in, down, up, *refs):
    quarters, (field, feats, cot, occ, sems) = refs[:4], refs[4:]
    copies = start_inputs(feats_in, cot_in, occ_in, feats, cot, occ, sems)
    lane = ints((512, 256), 1)
    rim = lane % 128
    wanted = rim // 16 * 64 + rim // 8 % 2 * 8 + rim % 8 + jnp.where(lane < 128, 48, 0)
    picks = jnp.where(ints((512, 256), 0) == wanted, 1.0, 0.0).astype(BF16)
    mask_inputs(copies, feats, cot, occ, field)
    rims = jnp.dot(field[...], picks, preferred_element_type=F32).astype(BF16)
    down[...] = rims[:, 0:128]
    up[...] = rims[:, 128:256]
    for number in range(4):
        quarters[number][...] = field[:, number * 128 : (number + 1) * 128]


def slab_kernel(after, first, last, ym, yp, left, right):
    blank = jnp.zeros((ROWS, 64), BF16)
    left[:, 0:128] = last[...]
    left[:, 128:256] = jnp.concatenate([ym[:, 96:128], yp[:, 96:128], blank], axis=1)
    right[:, 0:128] = first[...]
    right[:, 128:256] = jnp.concatenate([ym[:, 0:32], yp[:, 0:32], blank], axis=1)


def tap_blocks():
    for number in range(9):
        for dz in range(3):
            k = number * 3 + dz
            yield k, slice(dz * C, (dz + 1) * C), slice(number * C, (number + 1) * C)


def forward_weight(weight, out):
    whole = weight[...]
    for k, rows, columns in tap_blocks():
        out[rows, columns] = whole[:, k * C : (k + 1) * C]


def turned_weight(weight, out):
    across = weight[...].astype(F32).T.astype(BF16)
    for k, rows, columns in tap_blocks():
        out[rows, columns] = across[(26 - k) * C : (27 - k) * C, :]


def start_weights(first_in, second_in, first, second, sems):
    copies = [
        pltpu.make_async_copy(first_in, first, sems.at[0]),
        pltpu.make_async_copy(second_in, second, sems.at[1]),
    ]
    for copy in copies:
        copy.start()
    return copies


def late_weight_kernel(after, first_in, second_in, second_forward, first_turned, first, second, sems):
    copies = start_weights(first_in, second_in, first, second, sems)
    copies[1].wait()
    forward_weight(second, second_forward)
    copies[0].wait()
    turned_weight(first, first_turned)


def shifted_columns(source, columns, length):
    for number in range(9):
        start = (number // 3) * PAD * PAD + (number % 3) * PAD
        columns[number * C : (number + 1) * C, 0:length] = source[:, start : start + length]


def three_taps(weight, columns, length):
    parts = jnp.dot(weight[...], columns[:, 0:length], preferred_element_type=F32)
    return (
        parts[0:C]
        + pltpu.roll(parts[C : 2 * C], length - 1, 1)
        + pltpu.roll(parts[2 * C :], length - 2, 1)
    )


def weight_grad(gradient, columns, grads, tiles):
    stack = jnp.concatenate(
        [gradient, pltpu.roll(gradient, 1, 1), pltpu.roll(gradient, 2, 1)], axis=0
    ).astype(BF16)
    sums = lax.dot_general(
        stack, columns, (((1,), (1,)), ((), ())), preferred_element_type=F32
    ) * (1.0 / 512.0)
    for number in range(9):
        for dz in range(3):
            k = number * 3 + dz
            grads[:, k * C : (k + 1) * C] = sums[
                dz * C : (dz + 1) * C, number * C : (number + 1) * C
            ]
    grads[:, 27 * C :] = jnp.zeros((C, TILES_L * 128 - 27 * C), F32)
    for tile in range(6 * TILES_L):
        row, lane = tile // TILES_L * 16, tile % TILES_L * 128
        tiles[tile] = grads[row : row + 16, lane : lane + 128]
    tiles[6 * TILES_L :] = jnp.zeros((128 - 6 * TILES_L, 16, 128), F32)


def relative_owners(adj, own):
    owners = [adj[0, k] for k in range(27)]
    return [jnp.where(block < 0, 99, block // REPS - own[0]) for block in owners]


def among(relative, steps):
    found = relative[0] == steps[0]
    for value in relative:
        for step in steps:
            found = jnp.logical_or(found, value == step)
    return found


def early_weight_kernel(after, first_in, second_in, first_forward, second_turned, first, second, sems):
    copies = start_weights(first_in, second_in, first, second, sems)
    copies[0].wait()
    forward_weight(first, first_forward)
    copies[1].wait()
    turned_weight(second, second_turned)


def site_kernel(adj, own, places, low, side):
    relative = relative_owners(adj, own)
    from_left = among(relative, [-1 - GRID, -1, -1 + GRID])
    side[...] = jnp.full(side.shape, jnp.where(from_left, 1.0, 0.0), F32).astype(BF16)
    from_low = among(relative, [-GRID])
    low[...] = jnp.full(low.shape, jnp.where(from_low, 1.0, 0.0), F32).astype(BF16)
    p = ints((1, LANES), 1)
    at = [p // (PAD * PAD) - 2, p // PAD % PAD - 2, p % PAD - 2]
    out = [jnp.where(v < 0, 0, jnp.where(v >= BE, 2, 1)) for v in at]
    site = jnp.where(p < PAD**3, out[0] * 9 + out[1] * 3 + out[2], 27)
    x, y, z = (jnp.where(v < 0, v + BE, jnp.where(v >= BE, v - BE, v)) for v in at)
    which = jnp.full((1, LANES), 99, jnp.int32)
    for k in range(27):
        which = jnp.where(site == k, relative[k], which)
    place = jnp.where(which == 0, x * 64 + y * 8 + z, -1)
    for sx, sy in DIRECTIONS:
        nx, ny = (x - 6 if sx < 0 else x), (y - 6 if sy < 0 else y)
        if sx == 0:
            there = 512 + x * 16 + ny * 8 + z
        elif sy == 0:
            there = 640 + nx * 64 + y * 8 + z
        else:
            there = (768 if sy < 0 else 800) + nx * 16 + ny * 8 + z
        place = jnp.where(which == sx + GRID * sy, there, place)
    places[...] = jnp.broadcast_to(place, places.shape)


def either(flag, one, other):
    return one * flag + other * (1.0 - flag.astype(F32)).astype(BF16)


def place_kernel(q0, q1, q2, q3, ym, yp, places, low, base, hot_x, sources):
    for number, quarter in enumerate((q0, q1, q2, q3)):
        sources[:, number * 128 : (number + 1) * 128] = quarter[...]
    sources[:, 512:640] = either(low[0:1, :], ym[...], yp[...])
    width = 384
    for part in range(LANES // width):
        cut = slice(part * width, (part + 1) * width)
        hot = jnp.where(ints((896, width), 0) == places[0:1, cut], 1.0, 0.0).astype(BF16)
        hot_x[:, cut] = hot[640:896]
        base[:, cut] = jnp.dot(
            sources[...], hot[0:640], preferred_element_type=F32
        ).astype(BF16)


def main_kernel(
    own, xm, xp, base, hot_x, side, w_one, w_two,
    send, padded, hidden, grad_one, inner, columns,
    col_g, grads,
):
    slab = either(side[0:1, :], xm[...], xp[...])
    width = 384
    for part in range(LANES // width):
        cut = slice(part * width, (part + 1) * width)
        near = jnp.dot(slab, hot_x[:, cut], preferred_element_type=F32)
        padded[:, cut] = (base[:, cut].astype(F32) + near).astype(BF16)
    shifted_columns(padded[0:C, :], columns.at[0], OUTER)
    shifted_columns(padded[C : 2 * C, :], col_g, OUTER)
    mask = padded[2 * C : 2 * C + 1, BASE + 1 : BASE + 1 + OUTER].astype(F32)
    pre = three_taps(w_one, columns.at[0], OUTER)
    sig = jax.nn.sigmoid(pre)
    hidden[...] = (pre * sig * mask).astype(BF16)
    back = three_taps(w_two, col_g, OUTER)
    grad = (back * mask * sig * (1.0 + pre * (1.0 - sig))).astype(BF16)
    grad_one[...] = grad
    shifted_columns(hidden[...], columns.at[1], INNER)
    columns[1, :, INNER:OUTER] = jnp.zeros((9 * C, OUTER - INNER), BF16)
    kept = jnp.where(own_voxels(BASE + 1, OUTER), 1.0, 0.0)
    inner[0] = (grad.astype(F32) * kept).astype(BF16)
    start = 2 * (BASE + 1)
    kept = jnp.where(own_voxels(start, INNER), 1.0, 0.0)
    grad_two = padded[C : 2 * C, start : start + INNER].astype(F32)
    inner[1, :, 0:INNER] = (grad_two * kept).astype(BF16)
    inner[1, :, INNER:OUTER] = jnp.zeros((C, OUTER - INNER), BF16)
    weight_grad(inner[1 - own[1]].astype(F32), columns[1 - own[1]], grads, send)


def keep_kernel(own, inner, columns, keep, grads):
    weight_grad(inner[own[1]].astype(F32), columns[own[1]], grads, keep)


def out_kernel(after, padded, hidden, grad_one, w_two, w_one, out_feats, grad_feats, done, columns):
    done[...] = jnp.zeros((8, 128), F32)
    voxel = ints((INNER, 512), 1)
    inner = voxel // 64 * (PAD * PAD) + voxel // 8 % 8 * PAD + voxel % 8
    squeeze = jnp.where(ints((INNER, 512), 0) == inner, 1.0, 0.0).astype(BF16)
    start = 2 * (BASE + 1)
    mask = padded[2 * C : 2 * C + 1, start : start + INNER].astype(F32)
    for first, field, weight, out in (
        (0, hidden, w_two, out_feats),
        (C, grad_one, w_one, grad_feats),
    ):
        shifted_columns(field[...], columns, INNER)
        pre = three_taps(weight, columns, INNER)
        kept = padded[first : first + C, start : start + INNER].astype(F32)
        wide = (kept + pre * mask).astype(BF16)
        out[0] = jnp.dot(wide, squeeze, preferred_element_type=F32).astype(BF16)


def pair_kernel(keep, other, coded):
    for number in range(32):
        tiles = slice(number * 4, number * 4 + 4)
        total = keep[tiles] + other[tiles]
        most = jnp.maximum(jnp.max(jnp.abs(total), axis=1), 1e-30)
        exponent = jnp.ceil(jnp.log2(most))
        values = jnp.round(total * jnp.exp2(14.0 - exponent)[:, None, :])
        coded[number, 0:64] = values.astype(jnp.int32).astype(jnp.int16).reshape(64, 128)
        rows = jnp.concatenate([exponent, jnp.zeros((4, 128), F32)], axis=0)
        coded[number, 64:72] = rows.astype(jnp.int32).astype(jnp.int16)


def decode_kernel(coded, copies):
    total = jnp.zeros((4, 16, 128), F32)
    for number in range(32):
        exponent = coded[number, 64:72].astype(jnp.int32).astype(F32)[0:4]
        values = coded[number, 0:64].astype(jnp.int32).astype(F32).reshape(4, 16, 128)
        total = total + values * jnp.exp2(exponent - 14.0)[:, None, :]
    for number in range(copies.shape[0]):
        copies[number] = total.astype(BF16)


def share_kernel(count, parts, *refs):
    total = parts[0].astype(F32)
    for number in range(1, count):
        total = total + parts[number].astype(F32)
    copies = refs[-1]
    for number in range(copies.shape[0]):
        copies[number] = total.astype(BF16)


def write_half(half, out, rows, sems):
    copies = []
    for row in range(6):
        for lane in range(TILES_L):
            last = min((lane + 1) * 128, 27 * C)
            part = half[row * TILES_L + lane].astype(F32)
            rows[row * 16 : row * 16 + 16, lane * 128 : last] = part[:, : last - lane * 128]
        at = pl.ds(row * 16, 16)
        copies.append(pltpu.make_async_copy(rows.at[at], out.at[at], sems.at[row]))
        copies[-1].start()
    for copy in copies:
        copy.wait()


def mine_kernel(own, half, first, second, rows, sems):
    @pl.when(own[1] == 0)
    def _():
        write_half(half, first, rows, sems)

    @pl.when(own[1] != 0)
    def _():
        write_half(half, second, rows, sems)


def other_kernel(own, half, first_in, second_in, first, second, rows, sems):
    @pl.when(own[1] == 0)
    def _():
        write_half(half, second, rows, sems)

    @pl.when(own[1] != 0)
    def _():
        write_half(half, first, rows, sems)


VMEM = pl.BlockSpec(memory_space=pltpu.VMEM)
SMEM = pl.BlockSpec(memory_space=pltpu.SMEM)
HBM = pl.BlockSpec(memory_space=pltpu.HBM)
ANY = pl.BlockSpec(memory_space=pl.ANY)
DMA = pltpu.SemaphoreType.DMA
MIB = 1024 * 1024
PACK, EARLY, LATE = int(53.58 * MIB), int(52.6 * MIB), int(52.5 * MIB)


def call(kernel, outs, specs, scratch=(), place=VMEM, limit=40 * MIB, **options):
    return pl.pallas_call(
        kernel,
        out_shape=[jax.ShapeDtypeStruct(*out) for out in outs],
        in_specs=specs,
        out_specs=[place] * len(outs),
        scratch_shapes=scratch,
        compiler_params=pltpu.CompilerParams(vmem_limit_bytes=limit),
        **options,
    )


def from_owner(value, sx, sy):
    pairs = []
    for owner in range(GRID * GRID):
        column, row = owner % GRID + sx, owner // GRID + sy
        if 0 <= column < GRID and 0 <= row < GRID:
            pairs.append((row * GRID + column, owner))
    return lax.ppermute(value, ("zh", "zl", "y"), pairs)


def swap_halves(value):
    return lax.ppermute(value, "core", [(0, 1), (1, 0)])


def body(feats, cotangent, occupancy, counts, adjacency, w_first, w_second):
    own = jnp.stack([lax.axis_index(("zh", "zl", "y")), lax.axis_index("core")]).astype(jnp.int32)
    rim, slab, turned = ((ROWS, 128), BF16), ((ROWS, 256), BF16), ((3 * C, 9 * C), BF16)
    vmem = pltpu.VMEM
    inputs = [
        vmem((1, C, 512), BF16), vmem((1, C, 512), BF16), vmem((1, 512), jnp.int32), DMA((3,))
    ]
    weights = [vmem((C, 27 * C), BF16)] * 2 + [DMA((2,))]
    with jax.named_scope("pack"):
        down, up, *quarters = call(
            pack_kernel, [rim] * 6, [HBM] * 3, [vmem((ROWS, 512), BF16)] + inputs, limit=PACK
        )(feats, cotangent, occupancy)
    with jax.named_scope("sites"):
        places, low, side = call(
            site_kernel,
            [((8, LANES), jnp.int32), ((16, 128), BF16), ((16, 256), BF16)],
            [SMEM] * 2,
        )(adjacency, own)
    with jax.named_scope("rims_y"):
        ym, yp = from_owner(down, 0, -1), from_owner(up, 0, 1)
    with jax.named_scope("slabs"):
        left, right = call(slab_kernel, [slab, slab], [VMEM] * 5)(
            side, quarters[0], quarters[3], ym, yp
        )
    with jax.named_scope("rims_x"):
        xm, xp = from_owner(left, -1, 0), from_owner(right, 1, 0)
    with jax.named_scope("early_weights"):
        one_f, two_b = call(
            early_weight_kernel, [turned] * 2, [VMEM] + [HBM] * 2, weights, limit=EARLY
        )(left, w_first, w_second)
    with jax.named_scope("place"):
        base, hot_x = call(
            place_kernel,
            [((ROWS, LANES), BF16), ((256, LANES), BF16)],
            [VMEM] * 8,
            [vmem((ROWS, 640), BF16)],
        )(*quarters, ym, yp, places, low)
    half, grads = ((128, 16, 128), F32), vmem((C, TILES_L * 128), F32)
    outer = ((C, OUTER), BF16)
    with jax.named_scope("middle"):
        send, padded, hidden, grad_one, inner, columns = call(
            main_kernel,
            [
                half, ((ROWS, LANES), BF16), outer, outer,
                ((2, C, OUTER), BF16), ((2, 9 * C, OUTER), BF16),
            ],
            [SMEM] + [VMEM] * 7,
            [vmem((9 * C, OUTER), BF16), grads],
        )(own, xm, xp, base, hot_x, side, one_f, two_b)
    with jax.named_scope("keep"):
        (keep,) = call(keep_kernel, [half], [SMEM] + [VMEM] * 2, [grads])(own, inner, columns)
    with jax.named_scope("pair"):
        (coded,) = call(pair_kernel, [((32, 72, 128), jnp.int16)], [VMEM] * 2)(
            keep, swap_halves(send)
        )
    near, far = ("zl", "y", "x"), "zh"
    with jax.named_scope("sum"):
        parts = lax.all_to_all(coded, near, 0, 0)
        (copies,) = call(decode_kernel, [((8, 4, 16, 128), BF16)], [VMEM])(parts)
        parts = lax.all_to_all(copies, far, 0, 0)
    with jax.named_scope("late_weights"):
        two_f, one_b = call(
            late_weight_kernel, [turned] * 2, [ANY] + [HBM] * 2, weights, limit=LATE
        )(copies, w_first, w_second)
    with jax.named_scope("outputs"):
        out_feats, grad_feats, done = call(
            out_kernel,
            [((1, C, 512), BF16)] * 2 + [((8, 128), F32)],
            [ANY] + [VMEM] * 5,
            [vmem((9 * C, INNER), BF16)],
        )(copies, padded, hidden, grad_one, two_f, one_b)
    with jax.named_scope("shares"):
        (copies,) = call(
            lambda *refs: share_kernel(8, *refs), [((32, 4, 16, 128), BF16)], [VMEM] * 2
        )(parts, done)
        mine = lax.all_to_all(copies, near, 0, 0).reshape(128, 16, 128)
        other = swap_halves(mine)
    grad, rows = ((C, 27 * C), F32), [vmem((C, 27 * C), F32), DMA((6,))]
    with jax.named_scope("mine"):
        begun = call(mine_kernel, [grad] * 2, [SMEM, VMEM], rows, place=ANY)(own, mine)
    with jax.named_scope("other"):
        grad_first, grad_second = call(
            other_kernel, [grad] * 2, [SMEM, VMEM, ANY, ANY], rows, place=ANY,
            input_output_aliases={2: 0, 3: 1},
        )(own, other, *begun)
    return out_feats, grad_feats, grad_first, grad_second


def solution(mesh):
    fine = Mesh(mesh.devices.reshape(8, 2, 4, 4, 2), ("zh", "zl", "y", "x", "core"))
    both = ("zh", "zl", "y", "x", "core")
    blocks = P(both, None, None)
    rows = P(both, None)
    return jax.shard_map(
        body,
        mesh=fine,
        in_specs=(blocks, blocks, rows, rows, rows, P(), P()),
        out_specs=(blocks, blocks, P(), P()),
        check_vma=False,
    )
```

```python
import jax
import jax.numpy as jnp
import numpy as np
from jax import lax
from jax.experimental import pallas as pl
from jax.experimental.pallas import tpu as pltpu
from jax.sharding import Mesh, PartitionSpec as P

C = 96
BE = 8
GRID = 8
REPS = 8
ROWS = 208
PAD = 12
LANES = 1920
OUTER = 1536
INNER = 1152
SPAN = 384
BASE = PAD * PAD + PAD
TILES_L = 21
DIRECTIONS = [(-1, -1), (0, -1), (1, -1), (-1, 0), (1, 0), (-1, 1), (0, 1), (1, 1)]
OFFSETS = [(a, b, c) for a in (-1, 0, 1) for b in (-1, 0, 1) for c in (-1, 0, 1)]
F32, BF16 = jnp.float32, jnp.bfloat16


def ints(dims, axis):
    return lax.broadcasted_iota(jnp.int32, dims, axis)


def own_voxels(first, length):
    p = ints((1, length), 1) + first
    x, y, z = p // (PAD * PAD), p // PAD % PAD, p % PAD
    inside = [jnp.logical_and(at >= 2, at < 10) for at in (x, y, z)]
    return jnp.logical_and(jnp.logical_and(inside[0], inside[1]), inside[2])


def start_inputs(feats_in, cot_in, occ_in, feats, cot, occ, sems):
    copies = [
        pltpu.make_async_copy(source, target, sems.at[number])
        for number, (source, target) in enumerate(((occ_in, occ), (feats_in, feats), (cot_in, cot)))
    ]
    for copy in copies:
        copy.start()
    return copies


def mask_inputs(copies, feats, cot, occ, field):
    copies[0].wait()
    mask = (occ[...] != 0).astype(F32).astype(BF16)
    field[2 * C :, 0:512] = jnp.broadcast_to(mask, (ROWS - 2 * C, 512))
    copies[1].wait()
    field[0:C, 0:512] = feats[0] * mask
    copies[2].wait()
    field[C : 2 * C, 0:512] = cot[0] * mask


def pack_kernel(feats_in, cot_in, occ_in, down, up, *refs):
    quarters, (field, feats, cot, occ, sems) = refs[:4], refs[4:]
    copies = start_inputs(feats_in, cot_in, occ_in, feats, cot, occ, sems)
    lane = ints((512, 256), 1)
    rim = lane % 128
    wanted = rim // 16 * 64 + rim // 8 % 2 * 8 + rim % 8 + jnp.where(lane < 128, 48, 0)
    picks = jnp.where(ints((512, 256), 0) == wanted, 1.0, 0.0).astype(BF16)
    mask_inputs(copies, feats, cot, occ, field)
    rims = jnp.dot(field[...], picks, preferred_element_type=F32).astype(BF16)
    down[...] = rims[:, 0:128]
    up[...] = rims[:, 128:256]
    for number in range(4):
        quarters[number][...] = field[:, number * 128 : (number + 1) * 128]


def slab_kernel(after, first, last, ym, yp, left, right):
    blank = jnp.zeros((ROWS, 64), BF16)
    left[:, 0:128] = last[...]
    left[:, 128:256] = jnp.concatenate([ym[:, 96:128], yp[:, 96:128], blank], axis=1)
    right[:, 0:128] = first[...]
    right[:, 128:256] = jnp.concatenate([ym[:, 0:32], yp[:, 0:32], blank], axis=1)


def tap_blocks():
    for number in range(9):
        for dz in range(3):
            k = number * 3 + dz
            yield k, slice(dz * C, (dz + 1) * C), slice(number * C, (number + 1) * C)


def forward_weight(weight, out):
    whole = weight[...]
    for k, rows, columns in tap_blocks():
        out[rows, columns] = whole[:, k * C : (k + 1) * C]


def turned_weight(weight, out):
    across = weight[...].astype(F32).T.astype(BF16)
    for k, rows, columns in tap_blocks():
        out[rows, columns] = across[(26 - k) * C : (27 - k) * C, :]


def start_weights(first_in, second_in, first, second, sems):
    copies = [
        pltpu.make_async_copy(first_in, first, sems.at[0]),
        pltpu.make_async_copy(second_in, second, sems.at[1]),
    ]
    for copy in copies:
        copy.start()
    return copies


def late_weight_kernel(after, first_in, second_in, second_forward, first_turned, first, second, sems):
    copies = start_weights(first_in, second_in, first, second, sems)
    copies[1].wait()
    forward_weight(second, second_forward)
    copies[0].wait()
    turned_weight(first, first_turned)


def shifted_columns(source, columns, length):
    for number in range(9):
        start = (number // 3) * PAD * PAD + (number % 3) * PAD
        columns[number * C : (number + 1) * C, 0:length] = source[:, start : start + length]


def three_taps(weight, columns, length):
    parts = jnp.dot(weight[...], columns[:, 0:length], preferred_element_type=F32)
    return (
        parts[0:C]
        + pltpu.roll(parts[C : 2 * C], length - 1, 1)
        + pltpu.roll(parts[2 * C :], length - 2, 1)
    )


def weight_grad(gradient, columns, grads, tiles):
    stack = jnp.concatenate(
        [gradient, pltpu.roll(gradient, 1, 1), pltpu.roll(gradient, 2, 1)], axis=0
    ).astype(BF16)
    sums = lax.dot_general(
        stack, columns, (((1,), (1,)), ((), ())), preferred_element_type=F32
    ) * (1.0 / 512.0)
    for number in range(9):
        for dz in range(3):
            k = number * 3 + dz
            grads[:, k * C : (k + 1) * C] = sums[
                dz * C : (dz + 1) * C, number * C : (number + 1) * C
            ]
    grads[:, 27 * C :] = jnp.zeros((C, TILES_L * 128 - 27 * C), F32)
    for tile in range(6 * TILES_L):
        row, lane = tile // TILES_L * 16, tile % TILES_L * 128
        tiles[tile] = grads[row : row + 16, lane : lane + 128]
    tiles[6 * TILES_L :] = jnp.zeros((128 - 6 * TILES_L, 16, 128), F32)


def relative_owners(adj, own):
    owners = [adj[0, k] for k in range(27)]
    return [jnp.where(block < 0, 99, block // REPS - own[0]) for block in owners]


def among(relative, steps):
    found = relative[0] == steps[0]
    for value in relative:
        for step in steps:
            found = jnp.logical_or(found, value == step)
    return found


def early_weight_kernel(after, first_in, second_in, first_forward, second_turned, first, second, sems):
    copies = start_weights(first_in, second_in, first, second, sems)
    copies[0].wait()
    forward_weight(first, first_forward)
    copies[1].wait()
    turned_weight(second, second_turned)


def site_kernel(adj, own, places, low, side):
    relative = relative_owners(adj, own)
    from_left = among(relative, [-1 - GRID, -1, -1 + GRID])
    side[...] = jnp.full(side.shape, jnp.where(from_left, 1.0, 0.0), F32).astype(BF16)
    from_low = among(relative, [-GRID])
    low[...] = jnp.full(low.shape, jnp.where(from_low, 1.0, 0.0), F32).astype(BF16)
    p = ints((1, LANES), 1)
    at = [p // (PAD * PAD) - 2, p // PAD % PAD - 2, p % PAD - 2]
    out = [jnp.where(v < 0, 0, jnp.where(v >= BE, 2, 1)) for v in at]
    site = jnp.where(p < PAD**3, out[0] * 9 + out[1] * 3 + out[2], 27)
    x, y, z = (jnp.where(v < 0, v + BE, jnp.where(v >= BE, v - BE, v)) for v in at)
    which = jnp.full((1, LANES), 99, jnp.int32)
    for k in range(27):
        which = jnp.where(site == k, relative[k], which)
    place = jnp.where(which == 0, x * 64 + y * 8 + z, -1)
    for sx, sy in DIRECTIONS:
        nx, ny = (x - 6 if sx < 0 else x), (y - 6 if sy < 0 else y)
        if sx == 0:
            there = 512 + x * 16 + ny * 8 + z
        elif sy == 0:
            there = 640 + nx * 64 + y * 8 + z
        else:
            there = (768 if sy < 0 else 800) + nx * 16 + ny * 8 + z
        place = jnp.where(which == sx + GRID * sy, there, place)
    places[...] = jnp.broadcast_to(place, places.shape)


def either(flag, one, other):
    return one * flag + other * (1.0 - flag.astype(F32)).astype(BF16)


def place_kernel(
    q0, q1, q2, q3, ym, yp, places, low, w_one, w_two,
    base, hot_x, col_m, pre, back, sources, col_g,
):
    for number, quarter in enumerate((q0, q1, q2, q3)):
        sources[:, number * 128 : (number + 1) * 128] = quarter[...]
    sources[:, 512:640] = either(low[0:1, :], ym[...], yp[...])
    width = 384
    for part in range(LANES // width):
        cut = slice(part * width, (part + 1) * width)
        hot = jnp.where(ints((896, width), 0) == places[0:1, cut], 1.0, 0.0).astype(BF16)
        hot_x[:, cut] = hot[640:896]
        base[:, cut] = jnp.dot(
            sources[...], hot[0:640], preferred_element_type=F32
        ).astype(BF16)
    shifted_columns(base[0:C, :], col_m, OUTER)
    pre[...] = three_taps(w_one, col_m, OUTER)
    shifted_columns(base[C : 2 * C, :], col_g, OUTER)
    back[...] = three_taps(w_two, col_g, OUTER)


def main_kernel(
    own, xm, xp, base, hot_x, side, w_one, w_two, col_base, pre_base, back_base,
    send, padded, hidden, grad_one, inner, columns,
    near, col_w, wide_pre, wide_back, grads,
):
    from_left = jnp.max(side[...].astype(F32)) > 0.5
    start = pl.multiple_of(jnp.where(from_left, 0, OUTER - SPAN), 128)
    lanes, window = pl.ds(start, 2 * SPAN), pl.ds(start, SPAN)
    slab = either(side[0:1, :], xm[...], xp[...])
    near[...] = jnp.dot(slab, hot_x[:, lanes], preferred_element_type=F32).astype(BF16)
    padded[...] = base[...]
    padded[:, lanes] = base[:, lanes] + near[...]
    columns[0] = col_base[...]
    wide_pre[...] = pre_base[...]
    wide_back[...] = back_base[...]
    shifted_columns(near[0:C, :], col_w, SPAN)
    columns[0, :, window] = col_base[:, window] + col_w[...]
    wide_pre[:, window] = pre_base[:, window] + three_taps(w_one, col_w, SPAN)
    shifted_columns(near[C : 2 * C, :], col_w, SPAN)
    wide_back[:, window] = back_base[:, window] + three_taps(w_two, col_w, SPAN)
    mask = padded[2 * C : 2 * C + 1, BASE + 1 : BASE + 1 + OUTER].astype(F32)
    pre, back = wide_pre[...], wide_back[...]
    sig = jax.nn.sigmoid(pre)
    hidden[...] = (pre * sig * mask).astype(BF16)
    grad = (back * mask * sig * (1.0 + pre * (1.0 - sig))).astype(BF16)
    grad_one[...] = grad
    shifted_columns(hidden[...], columns.at[1], INNER)
    columns[1, :, INNER:OUTER] = jnp.zeros((9 * C, OUTER - INNER), BF16)
    kept = jnp.where(own_voxels(BASE + 1, OUTER), 1.0, 0.0)
    inner[0] = (grad.astype(F32) * kept).astype(BF16)
    start = 2 * (BASE + 1)
    kept = jnp.where(own_voxels(start, INNER), 1.0, 0.0)
    grad_two = padded[C : 2 * C, start : start + INNER].astype(F32)
    inner[1, :, 0:INNER] = (grad_two * kept).astype(BF16)
    inner[1, :, INNER:OUTER] = jnp.zeros((C, OUTER - INNER), BF16)
    weight_grad(inner[1 - own[1]].astype(F32), columns[1 - own[1]], grads, send)


def keep_kernel(own, inner, columns, keep, grads):
    weight_grad(inner[own[1]].astype(F32), columns[own[1]], grads, keep)


def out_kernel(after, padded, hidden, grad_one, w_two, w_one, out_feats, grad_feats, done, columns):
    done[...] = jnp.zeros((8, 128), F32)
    voxel = ints((INNER, 512), 1)
    inner = voxel // 64 * (PAD * PAD) + voxel // 8 % 8 * PAD + voxel % 8
    squeeze = jnp.where(ints((INNER, 512), 0) == inner, 1.0, 0.0).astype(BF16)
    start = 2 * (BASE + 1)
    mask = padded[2 * C : 2 * C + 1, start : start + INNER].astype(F32)
    for first, field, weight, out in (
        (0, hidden, w_two, out_feats),
        (C, grad_one, w_one, grad_feats),
    ):
        shifted_columns(field[...], columns, INNER)
        pre = three_taps(weight, columns, INNER)
        kept = padded[first : first + C, start : start + INNER].astype(F32)
        wide = (kept + pre * mask).astype(BF16)
        out[0] = jnp.dot(wide, squeeze, preferred_element_type=F32).astype(BF16)


def pair_kernel(keep, other, coded):
    for number in range(32):
        tiles = slice(number * 4, number * 4 + 4)
        total = keep[tiles] + other[tiles]
        most = jnp.maximum(jnp.max(jnp.abs(total), axis=1), 1e-30)
        exponent = jnp.ceil(jnp.log2(most))
        values = jnp.round(total * jnp.exp2(14.0 - exponent)[:, None, :])
        coded[number, 0:4] = values.astype(jnp.int32).astype(jnp.int16)
        rows = jnp.concatenate([exponent, jnp.zeros((12, 128), F32)], axis=0)
        coded[number, 4] = rows.astype(jnp.int32).astype(jnp.int16)


def decode_kernel(coded, copies):
    total = jnp.zeros((4, 16, 128), F32)
    for number in range(32):
        exponent = coded[number, 4].astype(jnp.int32).astype(F32)[0:4]
        values = coded[number, 0:4].astype(jnp.int32).astype(F32)
        total = total + values * jnp.exp2(exponent - 14.0)[:, None, :]
    for number in range(copies.shape[0]):
        copies[number] = total.astype(BF16)


def share_kernel(count, parts, *refs):
    total = parts[0].astype(F32)
    for number in range(1, count):
        total = total + parts[number].astype(F32)
    copies = refs[-1]
    for number in range(copies.shape[0]):
        copies[number] = total.astype(BF16)


def write_half(half, out, rows, sems):
    copies = []
    for row in range(6):
        for lane in range(TILES_L):
            last = min((lane + 1) * 128, 27 * C)
            part = half[row * TILES_L + lane].astype(F32)
            rows[row * 16 : row * 16 + 16, lane * 128 : last] = part[:, : last - lane * 128]
        at = pl.ds(row * 16, 16)
        copies.append(pltpu.make_async_copy(rows.at[at], out.at[at], sems.at[row]))
        copies[-1].start()
    for copy in copies:
        copy.wait()


def mine_kernel(own, half, first, second, rows, sems):
    @pl.when(own[1] == 0)
    def _():
        write_half(half, first, rows, sems)

    @pl.when(own[1] != 0)
    def _():
        write_half(half, second, rows, sems)


def other_kernel(own, half, first_in, second_in, first, second, rows, sems):
    @pl.when(own[1] == 0)
    def _():
        write_half(half, second, rows, sems)

    @pl.when(own[1] != 0)
    def _():
        write_half(half, first, rows, sems)


VMEM = pl.BlockSpec(memory_space=pltpu.VMEM)
SMEM = pl.BlockSpec(memory_space=pltpu.SMEM)
HBM = pl.BlockSpec(memory_space=pltpu.HBM)
ANY = pl.BlockSpec(memory_space=pl.ANY)
DMA = pltpu.SemaphoreType.DMA
MIB = 1024 * 1024
PACK, EARLY, LATE = int(53.58 * MIB), int(52.6 * MIB), int(52.5 * MIB)


def call(kernel, outs, specs, scratch=(), place=VMEM, limit=40 * MIB, **options):
    return pl.pallas_call(
        kernel,
        out_shape=[jax.ShapeDtypeStruct(*out) for out in outs],
        in_specs=specs,
        out_specs=[place] * len(outs),
        scratch_shapes=scratch,
        compiler_params=pltpu.CompilerParams(vmem_limit_bytes=limit),
        **options,
    )


def from_owner(value, sx, sy):
    pairs = []
    for owner in range(GRID * GRID):
        column, row = owner % GRID + sx, owner // GRID + sy
        if 0 <= column < GRID and 0 <= row < GRID:
            pairs.append((row * GRID + column, owner))
    return lax.ppermute(value, ("zh", "zl", "y"), pairs)


def swap_halves(value):
    return lax.ppermute(value, "core", [(0, 1), (1, 0)])


def body(feats, cotangent, occupancy, counts, adjacency, w_first, w_second):
    own = jnp.stack([lax.axis_index(("zh", "zl", "y")), lax.axis_index("core")]).astype(jnp.int32)
    rim, slab, turned = ((ROWS, 128), BF16), ((ROWS, 256), BF16), ((3 * C, 9 * C), BF16)
    vmem = pltpu.VMEM
    inputs = [
        vmem((1, C, 512), BF16), vmem((1, C, 512), BF16), vmem((1, 512), jnp.int32), DMA((3,))
    ]
    weights = [vmem((C, 27 * C), BF16)] * 2 + [DMA((2,))]
    with jax.named_scope("pack"):
        down, up, *quarters = call(
            pack_kernel, [rim] * 6, [HBM] * 3, [vmem((ROWS, 512), BF16)] + inputs, limit=PACK
        )(feats, cotangent, occupancy)
    with jax.named_scope("sites"):
        places, low, side = call(
            site_kernel,
            [((8, LANES), jnp.int32), ((16, 128), BF16), ((16, 256), BF16)],
            [SMEM] * 2,
        )(adjacency, own)
    with jax.named_scope("rims_y"):
        ym, yp = from_owner(down, 0, -1), from_owner(up, 0, 1)
    with jax.named_scope("slabs"):
        left, right = call(slab_kernel, [slab, slab], [VMEM] * 5)(
            side, quarters[0], quarters[3], ym, yp
        )
    with jax.named_scope("rims_x"):
        xm, xp = from_owner(left, -1, 0), from_owner(right, 1, 0)
    with jax.named_scope("early_weights"):
        one_f, two_b = call(
            early_weight_kernel, [turned] * 2, [VMEM] + [HBM] * 2, weights, limit=EARLY
        )(left, w_first, w_second)
    with jax.named_scope("place"):
        outer, field = ((C, OUTER), BF16), ((C, OUTER), F32)
        base, hot_x, col_base, pre_base, back_base = call(
            place_kernel,
            [((ROWS, LANES), BF16), ((256, LANES), BF16), ((9 * C, OUTER), BF16), field, field],
            [VMEM] * 10,
            [vmem((ROWS, 640), BF16), vmem((9 * C, OUTER), BF16)],
        )(*quarters, ym, yp, places, low, one_f, two_b)
    half, grads = ((128, 16, 128), F32), vmem((C, TILES_L * 128), F32)
    with jax.named_scope("middle"):
        send, padded, hidden, grad_one, inner, columns = call(
            main_kernel,
            [
                half, ((ROWS, LANES), BF16), outer, outer,
                ((2, C, OUTER), BF16), ((2, 9 * C, OUTER), BF16),
            ],
            [SMEM] + [VMEM] * 10,
            [
                vmem((ROWS, 2 * SPAN), BF16), vmem((9 * C, SPAN), BF16),
                vmem((C, OUTER), F32), vmem((C, OUTER), F32), grads,
            ],
            limit=24 * MIB,
        )(
            own, xm, xp, base, hot_x, side, one_f, two_b,
            col_base, pre_base, back_base,
        )
    with jax.named_scope("keep"):
        (keep,) = call(keep_kernel, [half], [SMEM] + [VMEM] * 2, [grads])(own, inner, columns)
    with jax.named_scope("pair"):
        (coded,) = call(pair_kernel, [((32, 5, 16, 128), jnp.int16)], [VMEM] * 2)(
            keep, swap_halves(send)
        )
    near, far = ("zl", "y", "x"), "zh"
    with jax.named_scope("sum"):
        parts = lax.all_to_all(coded, near, 0, 0)
        (copies,) = call(decode_kernel, [((8, 4, 16, 128), BF16)], [VMEM])(parts)
        parts = lax.all_to_all(copies, far, 0, 0)
    with jax.named_scope("late_weights"):
        two_f, one_b = call(
            late_weight_kernel, [turned] * 2, [ANY] + [HBM] * 2, weights, limit=LATE
        )(copies, w_first, w_second)
    with jax.named_scope("outputs"):
        out_feats, grad_feats, done = call(
            out_kernel,
            [((1, C, 512), BF16)] * 2 + [((8, 128), F32)],
            [ANY] + [VMEM] * 5,
            [vmem((9 * C, INNER), BF16)],
        )(copies, padded, hidden, grad_one, two_f, one_b)
    with jax.named_scope("shares"):
        (copies,) = call(
            lambda *refs: share_kernel(8, *refs), [((32, 4, 16, 128), BF16)], [VMEM] * 2
        )(parts, done)
        mine = lax.all_to_all(copies, near, 0, 0).reshape(128, 16, 128)
        other = swap_halves(mine)
    grad, rows = ((C, 27 * C), F32), [vmem((C, 27 * C), F32), DMA((6,))]
    with jax.named_scope("mine"):
        begun = call(mine_kernel, [grad] * 2, [SMEM, VMEM], rows, place=ANY)(own, mine)
    with jax.named_scope("other"):
        grad_first, grad_second = call(
            other_kernel, [grad] * 2, [SMEM, VMEM, ANY, ANY], rows, place=ANY,
            input_output_aliases={2: 0, 3: 1},
        )(own, other, *begun)
    return out_feats, grad_feats, grad_first, grad_second


def solution(mesh):
    fine = Mesh(mesh.devices.reshape(8, 2, 4, 4, 2), ("zh", "zl", "y", "x", "core"))
    both = ("zh", "zl", "y", "x", "core")
    blocks = P(both, None, None)
    rows = P(both, None)
    return jax.shard_map(
        body,
        mesh=fine,
        in_specs=(blocks, blocks, rows, rows, rows, P(), P()),
        out_specs=(blocks, blocks, P(), P()),
        check_vma=False,
    )
```

```python
import jax
import jax.numpy as jnp
import numpy as np
from jax import lax
from jax.experimental import pallas as pl
from jax.experimental.pallas import tpu as pltpu
from jax.sharding import Mesh, PartitionSpec as P

C = 96
BE = 8
GRID = 8
REPS = 8
ROWS = 208
PAD = 12
LANES = 1920
OUTER = 1536
INNER = 1152
BASE = PAD * PAD + PAD
TILES_L = 21
DIRECTIONS = [(-1, -1), (0, -1), (1, -1), (-1, 0), (1, 0), (-1, 1), (0, 1), (1, 1)]
OFFSETS = [(a, b, c) for a in (-1, 0, 1) for b in (-1, 0, 1) for c in (-1, 0, 1)]
F32, BF16 = jnp.float32, jnp.bfloat16


def ints(dims, axis):
    return lax.broadcasted_iota(jnp.int32, dims, axis)


def own_voxels(first, length):
    p = ints((1, length), 1) + first
    x, y, z = p // (PAD * PAD), p // PAD % PAD, p % PAD
    inside = [jnp.logical_and(at >= 2, at < 10) for at in (x, y, z)]
    return jnp.logical_and(jnp.logical_and(inside[0], inside[1]), inside[2])


def start_inputs(feats_in, cot_in, occ_in, feats, cot, occ, sems):
    copies = [
        pltpu.make_async_copy(source, target, sems.at[number])
        for number, (source, target) in enumerate(((occ_in, occ), (feats_in, feats), (cot_in, cot)))
    ]
    for copy in copies:
        copy.start()
    return copies


def mask_inputs(copies, feats, cot, occ, field):
    copies[0].wait()
    mask = (occ[...] != 0).astype(F32).astype(BF16)
    field[2 * C :, 0:512] = jnp.broadcast_to(mask, (ROWS - 2 * C, 512))
    copies[1].wait()
    field[0:C, 0:512] = feats[0] * mask
    copies[2].wait()
    field[C : 2 * C, 0:512] = cot[0] * mask


def pack_kernel(feats_in, cot_in, occ_in, down, up, *refs):
    quarters, (field, feats, cot, occ, sems) = refs[:4], refs[4:]
    copies = start_inputs(feats_in, cot_in, occ_in, feats, cot, occ, sems)
    lane = ints((512, 256), 1)
    rim = lane % 128
    wanted = rim // 16 * 64 + rim // 8 % 2 * 8 + rim % 8 + jnp.where(lane < 128, 48, 0)
    picks = jnp.where(ints((512, 256), 0) == wanted, 1.0, 0.0).astype(BF16)
    mask_inputs(copies, feats, cot, occ, field)
    rims = jnp.dot(field[...], picks, preferred_element_type=F32).astype(BF16)
    down[...] = rims[:, 0:128]
    up[...] = rims[:, 128:256]
    for number in range(4):
        quarters[number][...] = field[:, number * 128 : (number + 1) * 128]


def slab_kernel(after, first, last, ym, yp, left, right):
    blank = jnp.zeros((ROWS, 64), BF16)
    left[:, 0:128] = last[...]
    left[:, 128:256] = jnp.concatenate([ym[:, 96:128], yp[:, 96:128], blank], axis=1)
    right[:, 0:128] = first[...]
    right[:, 128:256] = jnp.concatenate([ym[:, 0:32], yp[:, 0:32], blank], axis=1)


def tap_blocks():
    for number in range(9):
        for dz in range(3):
            k = number * 3 + dz
            yield k, slice(dz * C, (dz + 1) * C), slice(number * C, (number + 1) * C)


def forward_weight(weight, out):
    whole = weight[...]
    for k, rows, columns in tap_blocks():
        out[rows, columns] = whole[:, k * C : (k + 1) * C]


def turned_weight(weight, out):
    across = weight[...].astype(F32).T.astype(BF16)
    for k, rows, columns in tap_blocks():
        out[rows, columns] = across[(26 - k) * C : (27 - k) * C, :]


def start_weights(first_in, second_in, first, second, sems):
    copies = [
        pltpu.make_async_copy(first_in, first, sems.at[0]),
        pltpu.make_async_copy(second_in, second, sems.at[1]),
    ]
    for copy in copies:
        copy.start()
    return copies


def late_weight_kernel(after, first_in, second_in, second_forward, first_turned, first, second, sems):
    copies = start_weights(first_in, second_in, first, second, sems)
    copies[1].wait()
    forward_weight(second, second_forward)
    copies[0].wait()
    turned_weight(first, first_turned)


def shifted_columns(source, columns, length):
    for number in range(9):
        start = (number // 3) * PAD * PAD + (number % 3) * PAD
        columns[number * C : (number + 1) * C, 0:length] = source[:, start : start + length]


def three_taps(weight, columns, length):
    parts = jnp.dot(weight[...], columns[:, 0:length], preferred_element_type=F32)
    return (
        parts[0:C]
        + pltpu.roll(parts[C : 2 * C], length - 1, 1)
        + pltpu.roll(parts[2 * C :], length - 2, 1)
    )


def weight_grad(gradient, columns, grads, tiles):
    stack = jnp.concatenate(
        [gradient, pltpu.roll(gradient, 1, 1), pltpu.roll(gradient, 2, 1)], axis=0
    ).astype(BF16)
    sums = lax.dot_general(
        stack, columns, (((1,), (1,)), ((), ())), preferred_element_type=F32
    ) * (1.0 / 512.0)
    for number in range(9):
        for dz in range(3):
            k = number * 3 + dz
            grads[:, k * C : (k + 1) * C] = sums[
                dz * C : (dz + 1) * C, number * C : (number + 1) * C
            ]
    grads[:, 27 * C :] = jnp.zeros((C, TILES_L * 128 - 27 * C), F32)
    for tile in range(6 * TILES_L):
        row, lane = tile // TILES_L * 16, tile % TILES_L * 128
        tiles[tile] = grads[row : row + 16, lane : lane + 128]
    tiles[6 * TILES_L :] = jnp.zeros((128 - 6 * TILES_L, 16, 128), F32)


def relative_owners(adj, own):
    owners = [adj[0, k] for k in range(27)]
    return [jnp.where(block < 0, 99, block // REPS - own[0]) for block in owners]


def among(relative, steps):
    found = relative[0] == steps[0]
    for value in relative:
        for step in steps:
            found = jnp.logical_or(found, value == step)
    return found


def prepare_kernel(
    adj, own, first_in, second_in, first_forward, second_turned, places, low, side,
    first, second, sems,
):
    copies = start_weights(first_in, second_in, first, second, sems)
    relative = relative_owners(adj, own)
    from_left = among(relative, [-1 - GRID, -1, -1 + GRID])
    side[...] = jnp.full(side.shape, jnp.where(from_left, 1.0, 0.0), F32).astype(BF16)
    from_low = among(relative, [-GRID])
    low[...] = jnp.full(low.shape, jnp.where(from_low, 1.0, 0.0), F32).astype(BF16)
    p = ints((1, LANES), 1)
    at = [p // (PAD * PAD) - 2, p // PAD % PAD - 2, p % PAD - 2]
    out = [jnp.where(v < 0, 0, jnp.where(v >= BE, 2, 1)) for v in at]
    site = jnp.where(p < PAD**3, out[0] * 9 + out[1] * 3 + out[2], 27)
    x, y, z = (jnp.where(v < 0, v + BE, jnp.where(v >= BE, v - BE, v)) for v in at)
    which = jnp.full((1, LANES), 99, jnp.int32)
    for k in range(27):
        which = jnp.where(site == k, relative[k], which)
    place = jnp.where(which == 0, x * 64 + y * 8 + z, -1)
    for sx, sy in DIRECTIONS:
        nx, ny = (x - 6 if sx < 0 else x), (y - 6 if sy < 0 else y)
        if sx == 0:
            there = 512 + x * 16 + ny * 8 + z
        elif sy == 0:
            there = 640 + nx * 64 + y * 8 + z
        else:
            there = (768 if sy < 0 else 800) + nx * 16 + ny * 8 + z
        place = jnp.where(which == sx + GRID * sy, there, place)
    places[...] = jnp.broadcast_to(place, places.shape)
    copies[0].wait()
    forward_weight(first, first_forward)
    copies[1].wait()
    turned_weight(second, second_turned)


def either(flag, one, other):
    return one * flag + other * (1.0 - flag.astype(F32)).astype(BF16)


def place_kernel(q0, q1, q2, q3, ym, yp, places, low, base, hot_x, sources):
    for number, quarter in enumerate((q0, q1, q2, q3)):
        sources[:, number * 128 : (number + 1) * 128] = quarter[...]
    sources[:, 512:640] = either(low[0:1, :], ym[...], yp[...])
    width = 384
    for part in range(LANES // width):
        cut = slice(part * width, (part + 1) * width)
        hot = jnp.where(ints((896, width), 0) == places[0:1, cut], 1.0, 0.0).astype(BF16)
        hot_x[:, cut] = hot[640:896]
        base[:, cut] = jnp.dot(
            sources[...], hot[0:640], preferred_element_type=F32
        ).astype(BF16)


def main_kernel(
    own, xm, xp, base, hot_x, side, w_one, w_two,
    send, padded, hidden, grad_one, inner, columns,
    col_g, grads,
):
    slab = either(side[0:1, :], xm[...], xp[...])
    width = 384
    for part in range(LANES // width):
        cut = slice(part * width, (part + 1) * width)
        near = jnp.dot(slab, hot_x[:, cut], preferred_element_type=F32)
        padded[:, cut] = (base[:, cut].astype(F32) + near).astype(BF16)
    shifted_columns(padded[0:C, :], columns.at[0], OUTER)
    shifted_columns(padded[C : 2 * C, :], col_g, OUTER)
    mask = padded[2 * C : 2 * C + 1, BASE + 1 : BASE + 1 + OUTER].astype(F32)
    pre = three_taps(w_one, columns.at[0], OUTER)
    sig = jax.nn.sigmoid(pre)
    hidden[...] = (pre * sig * mask).astype(BF16)
    back = three_taps(w_two, col_g, OUTER)
    grad = (back * mask * sig * (1.0 + pre * (1.0 - sig))).astype(BF16)
    grad_one[...] = grad
    shifted_columns(hidden[...], columns.at[1], INNER)
    columns[1, :, INNER:OUTER] = jnp.zeros((9 * C, OUTER - INNER), BF16)
    kept = jnp.where(own_voxels(BASE + 1, OUTER), 1.0, 0.0)
    inner[0] = (grad.astype(F32) * kept).astype(BF16)
    start = 2 * (BASE + 1)
    kept = jnp.where(own_voxels(start, INNER), 1.0, 0.0)
    grad_two = padded[C : 2 * C, start : start + INNER].astype(F32)
    inner[1, :, 0:INNER] = (grad_two * kept).astype(BF16)
    inner[1, :, INNER:OUTER] = jnp.zeros((C, OUTER - INNER), BF16)
    weight_grad(inner[1 - own[1]].astype(F32), columns[1 - own[1]], grads, send)


def keep_kernel(own, inner, columns, keep, grads):
    weight_grad(inner[own[1]].astype(F32), columns[own[1]], grads, keep)


def out_kernel(after, padded, hidden, grad_one, w_two, w_one, out_feats, grad_feats, done, columns):
    done[...] = jnp.zeros((8, 128), F32)
    voxel = ints((INNER, 512), 1)
    inner = voxel // 64 * (PAD * PAD) + voxel // 8 % 8 * PAD + voxel % 8
    squeeze = jnp.where(ints((INNER, 512), 0) == inner, 1.0, 0.0).astype(BF16)
    start = 2 * (BASE + 1)
    mask = padded[2 * C : 2 * C + 1, start : start + INNER].astype(F32)
    for first, field, weight, out in (
        (0, hidden, w_two, out_feats),
        (C, grad_one, w_one, grad_feats),
    ):
        shifted_columns(field[...], columns, INNER)
        pre = three_taps(weight, columns, INNER)
        kept = padded[first : first + C, start : start + INNER].astype(F32)
        wide = (kept + pre * mask).astype(BF16)
        out[0] = jnp.dot(wide, squeeze, preferred_element_type=F32).astype(BF16)


def pair_kernel(keep, other, coded):
    for number in range(32):
        tiles = slice(number * 4, number * 4 + 4)
        total = keep[tiles] + other[tiles]
        most = jnp.maximum(jnp.max(jnp.abs(total), axis=1), 1e-30)
        exponent = jnp.ceil(jnp.log2(most))
        values = jnp.round(total * jnp.exp2(14.0 - exponent)[:, None, :])
        coded[number, 0:4] = values.astype(jnp.int32).astype(jnp.int16)
        rows = jnp.concatenate([exponent, jnp.zeros((12, 128), F32)], axis=0)
        coded[number, 4] = rows.astype(jnp.int32).astype(jnp.int16)


def decode_kernel(coded, copies):
    total = jnp.zeros((4, 16, 128), F32)
    for number in range(32):
        exponent = coded[number, 4].astype(jnp.int32).astype(F32)[0:4]
        values = coded[number, 0:4].astype(jnp.int32).astype(F32)
        total = total + values * jnp.exp2(exponent - 14.0)[:, None, :]
    for number in range(copies.shape[0]):
        copies[number] = total.astype(BF16)


def share_kernel(count, parts, *refs):
    total = parts[0].astype(F32)
    for number in range(1, count):
        total = total + parts[number].astype(F32)
    copies = refs[-1]
    for number in range(copies.shape[0]):
        copies[number] = total.astype(BF16)


def write_half(half, out, rows, sems):
    copies = []
    for row in range(6):
        for lane in range(TILES_L):
            last = min((lane + 1) * 128, 27 * C)
            part = half[row * TILES_L + lane].astype(F32)
            rows[row * 16 : row * 16 + 16, lane * 128 : last] = part[:, : last - lane * 128]
        at = pl.ds(row * 16, 16)
        copies.append(pltpu.make_async_copy(rows.at[at], out.at[at], sems.at[row]))
        copies[-1].start()
    for copy in copies:
        copy.wait()


def mine_kernel(own, half, first, second, rows, sems):
    @pl.when(own[1] == 0)
    def _():
        write_half(half, first, rows, sems)

    @pl.when(own[1] != 0)
    def _():
        write_half(half, second, rows, sems)


def other_kernel(own, half, first_in, second_in, first, second, rows, sems):
    @pl.when(own[1] == 0)
    def _():
        write_half(half, second, rows, sems)

    @pl.when(own[1] != 0)
    def _():
        write_half(half, first, rows, sems)


VMEM = pl.BlockSpec(memory_space=pltpu.VMEM)
SMEM = pl.BlockSpec(memory_space=pltpu.SMEM)
HBM = pl.BlockSpec(memory_space=pltpu.HBM)
ANY = pl.BlockSpec(memory_space=pl.ANY)
DMA = pltpu.SemaphoreType.DMA
MIB = 1024 * 1024
PACK, PREPARE, LATE = int(53.58 * MIB), int(52.4 * MIB), int(52.5 * MIB)


def call(kernel, outs, specs, scratch=(), place=VMEM, limit=40 * MIB, **options):
    return pl.pallas_call(
        kernel,
        out_shape=[jax.ShapeDtypeStruct(*out) for out in outs],
        in_specs=specs,
        out_specs=[place] * len(outs),
        scratch_shapes=scratch,
        compiler_params=pltpu.CompilerParams(vmem_limit_bytes=limit),
        **options,
    )


def from_owner(value, sx, sy):
    pairs = []
    for owner in range(GRID * GRID):
        column, row = owner % GRID + sx, owner // GRID + sy
        if 0 <= column < GRID and 0 <= row < GRID:
            pairs.append((row * GRID + column, owner))
    return lax.ppermute(value, ("zh", "zl", "y"), pairs)


def swap_halves(value):
    return lax.ppermute(value, "core", [(0, 1), (1, 0)])


def body(feats, cotangent, occupancy, counts, adjacency, w_first, w_second):
    own = jnp.stack([lax.axis_index(("zh", "zl", "y")), lax.axis_index("core")]).astype(jnp.int32)
    rim, slab, turned = ((ROWS, 128), BF16), ((ROWS, 256), BF16), ((3 * C, 9 * C), BF16)
    vmem = pltpu.VMEM
    inputs = [
        vmem((1, C, 512), BF16), vmem((1, C, 512), BF16), vmem((1, 512), jnp.int32), DMA((3,))
    ]
    weights = [vmem((C, 27 * C), BF16)] * 2 + [DMA((2,))]
    with jax.named_scope("pack"):
        down, up, *quarters = call(
            pack_kernel, [rim] * 6, [HBM] * 3, [vmem((ROWS, 512), BF16)] + inputs, limit=PACK
        )(feats, cotangent, occupancy)
    with jax.named_scope("prepare"):
        one_f, two_b, places, low, side = call(
            prepare_kernel,
            [turned] * 2
            + [((8, LANES), jnp.int32), ((16, 128), BF16), ((16, 256), BF16)],
            [SMEM] * 2 + [HBM] * 2,
            weights,
            limit=PREPARE,
        )(adjacency, own, w_first, w_second)
    with jax.named_scope("rims_y"):
        ym, yp = from_owner(down, 0, -1), from_owner(up, 0, 1)
    with jax.named_scope("slabs"):
        left, right = call(slab_kernel, [slab, slab], [VMEM] * 5)(
            side, quarters[0], quarters[3], ym, yp
        )
    with jax.named_scope("rims_x"):
        xm, xp = from_owner(left, -1, 0), from_owner(right, 1, 0)
    with jax.named_scope("place"):
        base, hot_x = call(
            place_kernel,
            [((ROWS, LANES), BF16), ((256, LANES), BF16)],
            [VMEM] * 8,
            [vmem((ROWS, 640), BF16)],
        )(*quarters, ym, yp, places, low)
    half, grads = ((128, 16, 128), F32), vmem((C, TILES_L * 128), F32)
    outer = ((C, OUTER), BF16)
    with jax.named_scope("middle"):
        send, padded, hidden, grad_one, inner, columns = call(
            main_kernel,
            [
                half, ((ROWS, LANES), BF16), outer, outer,
                ((2, C, OUTER), BF16), ((2, 9 * C, OUTER), BF16),
            ],
            [SMEM] + [VMEM] * 7,
            [vmem((9 * C, OUTER), BF16), grads],
        )(own, xm, xp, base, hot_x, side, one_f, two_b)
    with jax.named_scope("keep"):
        (keep,) = call(keep_kernel, [half], [SMEM] + [VMEM] * 2, [grads])(own, inner, columns)
    with jax.named_scope("pair"):
        (coded,) = call(pair_kernel, [((32, 5, 16, 128), jnp.int16)], [VMEM] * 2)(
            keep, swap_halves(send)
        )
    near, far = ("x", "y", "zl"), "zh"
    with jax.named_scope("sum"):
        parts = lax.all_to_all(coded, near, 0, 0)
        (copies,) = call(decode_kernel, [((8, 4, 16, 128), BF16)], [VMEM])(parts)
        parts = lax.all_to_all(copies, far, 0, 0)
    with jax.named_scope("late_weights"):
        two_f, one_b = call(
            late_weight_kernel, [turned] * 2, [ANY] + [HBM] * 2, weights, limit=LATE
        )(copies, w_first, w_second)
    with jax.named_scope("outputs"):
        out_feats, grad_feats, done = call(
            out_kernel,
            [((1, C, 512), BF16)] * 2 + [((8, 128), F32)],
            [ANY] + [VMEM] * 5,
            [vmem((9 * C, INNER), BF16)],
        )(copies, padded, hidden, grad_one, two_f, one_b)
    with jax.named_scope("shares"):
        (copies,) = call(
            lambda *refs: share_kernel(8, *refs), [((32, 4, 16, 128), BF16)], [VMEM] * 2
        )(parts, done)
        mine = lax.all_to_all(copies, near, 0, 0).reshape(128, 16, 128)
        other = swap_halves(mine)
    grad, rows = ((C, 27 * C), F32), [vmem((C, 27 * C), F32), DMA((6,))]
    with jax.named_scope("mine"):
        begun = call(mine_kernel, [grad] * 2, [SMEM, VMEM], rows, place=ANY)(own, mine)
    with jax.named_scope("other"):
        grad_first, grad_second = call(
            other_kernel, [grad] * 2, [SMEM, VMEM, ANY, ANY], rows, place=ANY,
            input_output_aliases={2: 0, 3: 1},
        )(own, other, *begun)
    return out_feats, grad_feats, grad_first, grad_second


def solution(mesh):
    fine = Mesh(mesh.devices.reshape(8, 2, 4, 4, 2), ("zh", "zl", "y", "x", "core"))
    both = ("zh", "zl", "y", "x", "core")
    blocks = P(both, None, None)
    rows = P(both, None)
    return jax.shard_map(
        body,
        mesh=fine,
        in_specs=(blocks, blocks, rows, rows, rows, P(), P()),
        out_specs=(blocks, blocks, P(), P()),
        check_vma=False,
    )
```
